32 devices in a mesh: gx: 2 (over x), gy: 4 (over z), gz: 4 (over y, core).
Axes of the slice: x: 2, y: 2, z: 4, core: 2. Of those that a mesh axis runs over, the one named last changes fastest.
Arguments:
- load_field: float32 [3, 32, 64, 512], P(None, 'gx', 'gy', 'gz'), may hold values from -6 to 6
- design: float32 [32, 64, 512], P('gx', 'gy', 'gz'), may hold values from 0 to 1
- solid_map: int32 [2, 4, 32], replicated, may hold values from 0 to 1, as said below
Outputs:
- displacement: float32 [3, 32, 64, 512], P(None, 'gx', 'gy', 'gz')
- sensitivity: float32 [32, 64, 512], P('gx', 'gy', 'gz')
- density: float32 [32, 64, 512], P('gx', 'gy', 'gz')
The draws below stay inside these ranges and needn't reach their ends.
Inputs may be any that keep to these rules, and one draw needn't show every extreme that they name: Brick [i, j, k] holds the elements of rows i * 16 to (i + 1) * 16 - 1 of each dimension in turn. For i < 1, every j and every aligned run of 8 bricks along the third dimension, the run at first index i and the same run at i + 1 hold exactly 8 solid bricks together. The run solid_map[0, 0, 0:8] is all solid.
All inputs are finite; a program needn't handle non-finite values.
Results may differ from the reference program's by a relative error of at most 0.0001.
Values sent between devices are 32-bit elements; how exact they have to be, the bound alone decides.
A program may use at most 64 MiB of HBM per device.

```python
import math
import jax
import jax.numpy as jnp
import numpy as np
from jax import lax

BRICK = 16
BRZ = 8
ITERS = 2
NX = 32
NY = 64
NZ = 512
GBX = 2
GBY = 4
GBZ = 32


def draw_solid_map(key, part):
    key_count, key_order = jax.random.split(key)
    pair_count = GBX // 2
    columns = GBZ // BRZ
    counts = jax.random.randint(key_count, (pair_count, GBY, columns), 0, BRZ + 1)
    counts = counts.at[0, 0, 0].set(BRZ)
    scores = jax.random.randint(key_order, (2, pair_count, GBY, columns, BRZ), 0, 1 << 20) * BRZ + jnp.arange(BRZ, dtype=jnp.int32)
    rank_order = jnp.argsort(jnp.argsort(scores, axis=-1), axis=-1)
    needed = jnp.stack([counts, BRZ - counts])[..., None]
    solid_flags = (rank_order < needed).astype(jnp.int32)
    return solid_flags.reshape(GBX, GBY, GBZ)


def block_scale(key, shape, cuts, least, largest):
    factor_of, own = 1.0, jax.random.fold_in(key, 6)
    for position, parts in cuts:
        steps = jnp.exp(jax.random.uniform(jax.random.fold_in(own, position), (parts,), jnp.float32, least / len(cuts), largest / len(cuts)))
        factor_of = factor_of * jnp.repeat(steps, shape[position] // parts).reshape([-1 if axis == position else 1 for axis in range(len(shape))])
    return factor_of


def bell_draw(own_key, dims, scale, reach, cuts=(), kind=jnp.bfloat16):
    values = jax.random.normal(own_key, dims, jnp.float32) * scale
    if len(cuts) > 0:
        values = block_scale(own_key, dims, cuts, -0.22, 0.18) * values
    return jnp.clip(values, min=-reach, max=reach).astype(kind)


def setup_inputs(seed: int = 0) -> dict:
    splits = jax.random.split(jax.random.key(seed), 4)
    return {
        "load_field": bell_draw(splits[0], (3, NX, NY, NZ), 1.0, 6.0, ((1, 2), (2, 4), (3, 4)), jnp.float32),
        "design": jnp.clip(1.0 * jax.random.uniform(splits[1], (NX, NY, NZ), jnp.float32) ** block_scale(splits[1], (NX, NY, NZ), ((0, 2), (1, 4), (2, 4)), -0.2, 0.2), 0.0, 1.0),
        "solid_map": draw_solid_map(jax.random.fold_in(splits[3], 71), 0),
    }


young_floor = 0.001
spring_rate = 0.05
sharpness = 8.0
threshold = 0.5
poisson = 0.3
precise = lax.Precision.HIGHEST

def element_matrix():
    lame_first = poisson / ((1.0 + poisson) * (1.0 - 2.0 * poisson))
    shear_mod = 1.0 / (2.0 * (1.0 + poisson))
    elastic = np.zeros((6, 6))
    elastic[:3, :3] = lame_first
    for axis_one in range(3):
        elastic[axis_one, axis_one] += 2.0 * shear_mod
        elastic[axis_one + 3, axis_one + 3] = shear_mod
    gauss_point = 1.0 / math.sqrt(3.0)
    stiffness = np.zeros((24, 24))
    for point_x in (-gauss_point, gauss_point):
        for point_y in (-gauss_point, gauss_point):
            for point_z in (-gauss_point, gauss_point):
                strain = np.zeros((6, 24))
                for corner in range(8):
                    sign_a = 2 * (corner // 4) - 1
                    sign_b = 2 * (corner // 2 % 2) - 1
                    sign_c = 2 * (corner % 2) - 1
                    along_x = 0.25 * sign_a * (1 + sign_b * point_y) * (1 + sign_c * point_z)
                    along_y = 0.25 * (1 + sign_a * point_x) * sign_b * (1 + sign_c * point_z)
                    along_z = 0.25 * (1 + sign_a * point_x) * (1 + sign_b * point_y) * sign_c
                    column = 3 * corner
                    strain[0, column] = along_x
                    strain[1, column + 1] = along_y
                    strain[2, column + 2] = along_z
                    strain[3, column + 1] = along_z
                    strain[3, column + 2] = along_y
                    strain[4, column] = along_z
                    strain[4, column + 2] = along_x
                    strain[5, column] = along_y
                    strain[5, column + 1] = along_x
                stiffness += strain.T @ elastic @ strain * 0.125
    return jnp.asarray(stiffness, dtype=jnp.float32)

def cone_offsets():
    listed = []
    for step_x in range(-2, 3):
        for step_y in range(-2, 3):
            for step_z in range(-2, 3):
                radius = step_x * step_x + step_y * step_y + step_z * step_z
                if radius < 9:
                    listed.append((step_x, step_y, step_z, 3.0 - math.sqrt(radius)))
    return listed

def corner_values(node_values, width_x, width_y, width_z):
    pieces = []
    for corner in range(8):
        shift_a, shift_b, shift_c = (corner // 4, corner // 2 % 2, corner % 2)
        pieces.append(node_values[:, shift_a:shift_a + width_x, shift_b:shift_b + width_y, shift_c:shift_c + width_z])
    return jnp.concatenate(pieces, 0).reshape(24, -1)

def spread_back(forces, width_x, width_y, width_z):
    forces = forces.reshape(24, width_x, width_y, width_z)
    summed = jnp.zeros((3, width_x + 1, width_y + 1, width_z + 1), jnp.float32)
    for corner in range(8):
        shift_a, shift_b, shift_c = (corner // 4, corner // 2 % 2, corner % 2)
        summed = summed + jnp.pad(forces[3 * corner:3 * corner + 3], ((0, 0), (shift_a, 1 - shift_a), (shift_b, 1 - shift_b), (shift_c, 1 - shift_c)))
    return summed

def corner_energy(stiffness, corner_vals):
    return lax.optimization_barrier(jnp.sum(corner_vals * jnp.dot(stiffness, corner_vals, precision=precise, preferred_element_type=jnp.float32), 0))

def reference(load_field, design, solid_map):
    stiffness = element_matrix()
    offsets = cone_offsets()

    def inside(length):
        coords = jnp.arange(length, dtype=jnp.int32)
        return {step_off: ((coords + step_off >= 0) & (coords + step_off < length)).astype(jnp.float32) for step_off in range(-2, 3)}
    inside_x, inside_y, inside_z = (inside(NX), inside(NY), inside(NZ))
    weight_sum = jnp.zeros((NX, NY, NZ), jnp.float32)
    for step_x, step_y, step_z, weight in offsets:
        weight_sum = weight_sum + weight * (inside_x[step_x][:, None, None] * inside_y[step_y][None, :, None] * inside_z[step_z][None, None, :])

    def cone_sum(values):
        extended = jnp.pad(values, 2)
        summed = jnp.zeros_like(values)
        for step_x, step_y, step_z, weight in offsets:
            summed = summed + weight * extended[2 + step_x:2 + step_x + NX, 2 + step_y:2 + step_y + NY, 2 + step_z:2 + step_z + NZ]
        return summed
    smoothed = cone_sum(design) / weight_sum
    lift_value = math.tanh(sharpness * threshold)
    scale_sum = lift_value + math.tanh(sharpness * (1.0 - threshold))
    tanh_shift = jnp.tanh(sharpness * (smoothed - threshold))
    density = (lift_value + tanh_shift) / scale_sum
    cell_flags = jnp.repeat(jnp.repeat(jnp.repeat(solid_map.astype(jnp.float32), BRICK, 0), BRICK, 1), BRICK, 2)
    moduli = (young_floor + density ** 3 * (1.0 - young_floor)) * cell_flags

    def operate(vector):
        padded = jnp.pad(vector, ((0, 0), (0, 1), (0, 1), (0, 1)))

        def slab_step(upper_prev, slab_index):
            node_values = lax.dynamic_slice_in_dim(padded, slab_index, 2, 1)
            slab_moduli = lax.dynamic_slice_in_dim(moduli, slab_index, 1, 0)
            corner_vals = corner_values(node_values, 1, NY, NZ)
            forces = jnp.dot(stiffness, corner_vals * slab_moduli.reshape(1, -1), precision=precise, preferred_element_type=jnp.float32)
            spread = spread_back(forces, 1, NY, NZ)
            plane = (upper_prev + spread[:, 0])[:, :NY, :NZ]
            return (spread[:, 1], plane)
        start_carry = jnp.zeros((3, NY + 1, NZ + 1), jnp.float32)
        _, planes = lax.scan(slab_step, start_carry, jnp.arange(NX, dtype=jnp.int32))
        return jnp.transpose(planes, (1, 0, 2, 3)) + spring_rate * vector
    displacement = jnp.zeros_like(load_field)
    residual = load_field
    direction = load_field
    norm_now = jnp.sum(residual * residual)
    for iteration in range(ITERS):
        applied = operate(direction)
        step_size = norm_now / jnp.sum(direction * applied)
        displacement = displacement + step_size * direction
        residual = residual - step_size * applied
        norm_next = jnp.sum(residual * residual)
        direction = residual + norm_next / norm_now * direction
        norm_now = norm_next
    padded_disp = jnp.pad(displacement, ((0, 0), (0, 1), (0, 1), (0, 1)))

    def slab_energy(slab_index):
        node_values = lax.dynamic_slice_in_dim(padded_disp, slab_index, 2, 1)
        corner_vals = corner_values(node_values, 1, NY, NZ)
        return corner_energy(stiffness, corner_vals).reshape(NY, NZ)
    energy = lax.map(slab_energy, jnp.arange(NX, dtype=jnp.int32))
    pushed = -3.0 * (1.0 - young_floor) * density ** 2 * cell_flags * energy * (sharpness * (1.0 - tanh_shift * tanh_shift) / scale_sum) / weight_sum
    sensitivity = cone_sum(pushed)
    return (displacement, sensitivity, density)
```

```python
import itertools
import math

import jax
import jax.numpy as jnp
import numpy as np
from jax import lax
from jax.experimental import pallas as pl
from jax.experimental.pallas import tpu as pltpu
from jax.sharding import PartitionSpec as P

BRICK = 16
HALO = 5
PAD = 8
LANES = 128

young_floor = 0.001
spring_rate = 0.05
sharpness = 8.0
threshold = 0.5
poisson = 0.3
MESH = pl.DeviceIdType.MESH


def element_matrix():
    lame_first = poisson / ((1.0 + poisson) * (1.0 - 2.0 * poisson))
    shear_mod = 1.0 / (2.0 * (1.0 + poisson))
    elastic = np.zeros((6, 6))
    elastic[:3, :3] = lame_first
    for axis_one in range(3):
        elastic[axis_one, axis_one] += 2.0 * shear_mod
        elastic[axis_one + 3, axis_one + 3] = shear_mod
    gauss_point = 1.0 / math.sqrt(3.0)
    stiffness = np.zeros((24, 24))
    for point_x in (-gauss_point, gauss_point):
        for point_y in (-gauss_point, gauss_point):
            for point_z in (-gauss_point, gauss_point):
                strain = np.zeros((6, 24))
                for corner in range(8):
                    sign_a = 2 * (corner // 4) - 1
                    sign_b = 2 * (corner // 2 % 2) - 1
                    sign_c = 2 * (corner % 2) - 1
                    along_x = 0.25 * sign_a * (1 + sign_b * point_y) * (1 + sign_c * point_z)
                    along_y = 0.25 * (1 + sign_a * point_x) * sign_b * (1 + sign_c * point_z)
                    along_z = 0.25 * (1 + sign_a * point_x) * (1 + sign_b * point_y) * sign_c
                    column = 3 * corner
                    strain[0, column] = along_x
                    strain[1, column + 1] = along_y
                    strain[2, column + 2] = along_z
                    strain[3, column + 1] = along_z
                    strain[3, column + 2] = along_y
                    strain[4, column] = along_z
                    strain[4, column + 2] = along_x
                    strain[5, column] = along_y
                    strain[5, column + 1] = along_x
                stiffness += strain.T @ elastic @ strain * 0.125
    return stiffness


def cone_offsets():
    listed = []
    for step_x in range(-2, 3):
        for step_y in range(-2, 3):
            for step_z in range(-2, 3):
                radius = step_x * step_x + step_y * step_y + step_z * step_z
                if radius < 9:
                    listed.append((step_x, step_y, step_z, 3.0 - math.sqrt(radius)))
    return listed


def modal_matrix():
    stiffness = element_matrix()
    change = np.zeros((24, 24))
    for mode in itertools.product((0, 1), repeat=3):
        for corner in itertools.product((0, 1), repeat=3):
            sign = 1.0
            for is_diff, side in zip(mode, corner):
                sign *= (2 * side - 1) if is_diff else 1
            for comp in range(3):
                row = 3 * (4 * mode[0] + 2 * mode[1] + mode[2]) + comp
                change[row, 3 * (4 * corner[0] + 2 * corner[1] + corner[2]) + comp] = sign
    modal = change @ stiffness @ change.T / 64.0
    modal[np.abs(modal) < 1e-10] = 0.0
    return modal


def cone_table():
    table = {}
    for step_x, step_y, step_z, weight in cone_offsets():
        if min(step_x, step_y, step_z) >= 0:
            table[(step_x, step_y, step_z)] = weight
    return table


MODES = tuple(itertools.product((0, 1), repeat=2))


def roll(value, shift, axis):
    return pltpu.roll(value, shift % value.shape[axis], axis)


def plane_modes(values, height, width):
    out = {}
    for comp, value in enumerate(values):
        ahead = roll(value, -1, 1)
        for mode_z, part in enumerate((value + ahead, ahead - value)):
            part = part[:, :width]
            above = roll(part, -1, 0)[:height]
            part = part[:height]
            out[(comp, 0, mode_z)] = part + above
            out[(comp, 1, mode_z)] = above - part
    return out


def modal_product(modal, modes):
    out = {}
    for row in range(24):
        total = None
        for col in range(24):
            if modal[row, col] != 0.0:
                term = modes[col] * float(modal[row, col])
                total = term if total is None else total + term
        out[row] = total
    return out


def key_row(mode_x, key):
    comp, mode_y, mode_z = key
    return 3 * (4 * mode_x + 2 * mode_y + mode_z) + comp


KEYS = tuple((comp, my, mz) for comp in range(3) for my, mz in MODES)


def element_modes(old, new):
    modes = {}
    for key in KEYS:
        modes[key_row(0, key)] = old[key] + new[key]
        modes[key_row(1, key)] = new[key] - old[key]
    return modes


def modal_energy(modal, modes):
    forces = modal_product(modal, modes)
    total = None
    for row in range(24):
        if forces[row] is not None:
            term = forces[row] * modes[row]
            total = term if total is None else total + term
    return total


def cone_planes(table, value, height, width):
    along_z = {
        0: value[:, :width],
        1: (roll(value, 1, 1) + roll(value, -1, 1))[:, :width],
        2: (roll(value, 2, 1) + roll(value, -2, 1))[:, :width],
    }
    sums = [None, None, None]
    for far_z, part in along_z.items():
        along_y = (
            part[:height],
            (roll(part, 1, 0) + roll(part, -1, 0))[:height],
            (roll(part, 2, 0) + roll(part, -2, 0))[:height],
        )
        for far_x in range(3):
            for far_y in range(3):
                weight = table.get((far_x, far_y, far_z))
                if weight is not None:
                    term = along_y[far_y] * weight
                    sums[far_x] = term if sums[far_x] is None else sums[far_x] + term
    return sums


def kernel(
    counts,
    load,
    design,
    solid,
    disp_out,
    sens_out,
    dens_out,
    field,
    applied,
    moduli,
    factor,
    flags,
    cone,
    pushed,
    held,
    carry,
    small_held,
    packed,
    arrived,
    masks,
    part_z,
    part_xy,
    face_send,
    face_recv,
    z_send,
    z_recv,
    xy_send,
    xy_recv,
):
    count_x, count_y, count_z = counts
    size_x, size_y, size_z = design.shape
    rows, lanes = size_y + 2 * PAD, size_z + LANES
    planes = size_x + 2 * HALO
    ix, iy, iz = lax.axis_index("gx"), lax.axis_index("gy"), lax.axis_index("gz")
    modal = modal_matrix()
    table = cone_table()
    f32 = jnp.float32

    def z_partner(step):
        return (ix, iy, lax.rem(iz + step, count_z))

    def xy_partner(step):
        spot = lax.rem(ix * count_y + iy + step, count_x * count_y)
        return (spot // count_y, lax.rem(spot, count_y), iz)

    def clear(plane, _):
        for index in range(4):
            field[index, plane, :, :size_z] = jnp.zeros((rows, size_z), f32)
        return 0

    lax.fori_loop(0, planes, clear, 0)
    arrived[...] = jnp.zeros_like(arrived)

    def place(plane, _):
        field[0, plane + HALO, :size_y, :size_z] = design[plane]
        for comp in range(3):
            field[comp + 1, plane + HALO, :size_y, :size_z] = load[comp, plane]
        return 0

    lax.fori_loop(0, size_x, place, 0)

    barrier = pltpu.get_barrier_semaphore()
    for step in range(1, count_z):
        pl.semaphore_signal(barrier, inc=1, device_id=z_partner(step), device_id_type=MESH)
    for step in range(1, count_x * count_y):
        pl.semaphore_signal(barrier, inc=1, device_id=xy_partner(step), device_id_type=MESH)
    pl.semaphore_wait(barrier, count_z - 1 + count_x * count_y - 1)

    def exchange(slot, down, up, down_id, up_id, has_down, has_up):
        to_down = pltpu.make_async_remote_copy(
            src_ref=down[0], dst_ref=down[1], send_sem=face_send.at[slot],
            recv_sem=face_recv.at[slot], device_id=down_id, device_id_type=MESH,
        )
        to_up = pltpu.make_async_remote_copy(
            src_ref=up[0], dst_ref=up[1], send_sem=face_send.at[slot + 1],
            recv_sem=face_recv.at[slot + 1], device_id=up_id, device_id_type=MESH,
        )

        @pl.when(has_down)
        def _():
            to_down.start()

        @pl.when(has_up)
        def _():
            to_up.start()

        @pl.when(has_up)
        def _():
            to_down.wait_recv()
            to_up.wait_send()

        @pl.when(has_down)
        def _():
            to_up.wait_recv()
            to_down.wait_send()

    inner = pl.ds(HALO, size_x)
    main = pl.ds(0, size_z)
    exchange(
        0,
        (field.at[:, inner, pl.ds(0, PAD), main], field.at[:, inner, pl.ds(size_y, PAD), main]),
        (
            field.at[:, inner, pl.ds(size_y - PAD, PAD), main],
            field.at[:, inner, pl.ds(size_y + PAD, PAD), main],
        ),
        (ix, lax.max(iy - 1, 0), iz),
        (ix, lax.min(iy + 1, count_y - 1), iz),
        iy > 0,
        iy < count_y - 1,
    )
    every = pl.ds(0, rows)
    exchange(
        2,
        (
            field.at[:, pl.ds(HALO, HALO), every, main],
            field.at[:, pl.ds(HALO + size_x, HALO), every, main],
        ),
        (field.at[:, pl.ds(size_x, HALO), every, main], field.at[:, pl.ds(0, HALO), every, main]),
        (lax.max(ix - 1, 0), iy, iz),
        (lax.min(ix + 1, count_x - 1), iy, iz),
        ix > 0,
        ix < count_x - 1,
    )

    lane_of = lax.broadcasted_iota(jnp.int32, (rows, LANES), 1)
    per_tile = LANES // PAD
    tiles = -(-planes // per_tile)

    def pack(index, _):
        for tile in range(tiles):
            low = jnp.zeros((rows, LANES), f32)
            high = jnp.zeros((rows, LANES), f32)
            for spot in range(min(per_tile, planes - tile * per_tile)):
                plane = tile * per_tile + spot
                here = (lane_of >= spot * PAD) & (lane_of < (spot + 1) * PAD)
                first = field[index, plane, :, :LANES]
                last = field[index, plane, :, size_z - LANES : size_z]
                low = jnp.where(here, roll(first, spot * PAD, 1), low)
                high = jnp.where(here, roll(last, (spot + 1) * PAD, 1), high)
            packed[0, index, tile] = low
            packed[1, index, tile] = high
        return 0

    lax.fori_loop(0, 4, pack, 0)
    exchange(
        4,
        (packed.at[0], arrived.at[0]),
        (packed.at[1], arrived.at[1]),
        (ix, iy, lax.max(iz - 1, 0)),
        (ix, iy, lax.min(iz + 1, count_z - 1)),
        iz > 0,
        iz < count_z - 1,
    )

    def unpack(index, _):
        for tile in range(tiles):
            above = arrived[0, index, tile]
            below = arrived[1, index, tile]
            for spot in range(min(per_tile, planes - tile * per_tile)):
                plane = tile * per_tile + spot
                value = jnp.where(lane_of < PAD, roll(above, -spot * PAD, 1), 0.0)
                value = jnp.where(
                    lane_of >= LANES - PAD, roll(below, -(spot + 1) * PAD, 1), value
                )
                field[index, plane, :, size_z:] = value
        return 0

    lax.fori_loop(0, 4, unpack, 0)

    row_at = lax.broadcasted_iota(jnp.int32, (rows, lanes), 0)
    lane_at = lax.broadcasted_iota(jnp.int32, (rows, lanes), 1)
    row_at = jnp.where(row_at < size_y + PAD, row_at, row_at - rows) + iy * size_y
    lane_at = jnp.where(lane_at < size_z + LANES // 2, lane_at, lane_at - lanes) + iz * size_z
    inside_yz = (
        (row_at >= 0) & (row_at < size_y * count_y) & (lane_at >= 0) & (lane_at < size_z * count_z)
    )
    masks[0] = jnp.where(inside_yz, 1.0, 0.0).astype(f32)
    for far_x, value in enumerate(cone_planes(table, masks[0], rows, lanes)):
        masks[1 + far_x] = value

    def inside_x(plane):
        where = plane + ix * size_x
        return jnp.where((where >= 0) & (where < size_x * count_x), 1.0, 0.0).astype(f32)

    bricks_x, bricks_y, bricks_z = size_x // BRICK, size_y // BRICK, size_z // BRICK
    lane8 = lax.broadcasted_iota(jnp.int32, (PAD, lanes), 1)

    def brick(bx, by, bz):
        gx, gy, gz = ix * bricks_x + bx, iy * bricks_y + by, iz * bricks_z + bz
        top_x, top_y, top_z = bricks_x * count_x, bricks_y * count_y, bricks_z * count_z
        good = (gx >= 0) & (gx < top_x) & (gy >= 0) & (gy < top_y) & (gz >= 0) & (gz < top_z)
        value = solid[
            lax.clamp(0, gx, top_x - 1), lax.clamp(0, gy, top_y - 1), lax.clamp(0, gz, top_z - 1)
        ]
        return value.astype(f32) * jnp.where(good, 1.0, 0.0).astype(f32)

    for bx in range(-1, bricks_x + 1):
        for by in range(-1, bricks_y + 1):
            line = jnp.zeros((PAD, lanes), f32)
            for bz in range(-1, bricks_z + 1):
                low, top = bz * BRICK, (bz + 1) * BRICK
                if bz < 0:
                    low, top = lanes - LANES // 2, lanes
                line = jnp.where((lane8 >= low) & (lane8 < top), brick(bx, by, bz), line)
            if by < 0:
                spots = [size_y + PAD]
            elif by == bricks_y:
                spots = [size_y]
            else:
                spots = range(by * BRICK, (by + 1) * BRICK, PAD)
            for spot in spots:
                flags[bx + 1, spot : spot + PAD, :] = line

    def filter_plane(plane, _):
        for far_x, value in enumerate(cone_planes(table, field[0, plane], rows, lanes)):
            cone[far_x, plane] = value
        return 0

    lax.fori_loop(0, planes, filter_plane, 0)
    lift = math.tanh(sharpness * threshold)
    scale = lift + math.tanh(sharpness * (1.0 - threshold))

    def gathered(source, plane):
        return (
            source[0, plane]
            + (source[1, plane - 1] + source[1, plane + 1])
            + (source[2, plane - 2] + source[2, plane + 2])
        )

    def material(step, _):
        at = step - 3
        plane = step + 2
        weight = inside_x(at) * masks[1]
        weight = weight + (inside_x(at - 1) + inside_x(at + 1)) * masks[2]
        weight = weight + (inside_x(at - 2) + inside_x(at + 2)) * masks[3]
        weight = 1.0 / jnp.maximum(weight, 1.0)
        tanh_shift = jnp.tanh(sharpness * (gathered(cone, plane) * weight - threshold))
        density = (lift + tanh_shift) * (1.0 / scale)
        flag = flags[(at + BRICK) // BRICK]
        squared = density * density
        moduli[step] = (young_floor + (1.0 - young_floor) * (squared * density)) * flag
        slope = (1.0 - tanh_shift * tanh_shift) * weight
        factor[step] = (
            (-3.0 * (1.0 - young_floor) * sharpness / scale) * (squared * flag) * slope
        )

        @pl.when((at >= 0) & (at < size_x))
        def _():
            dens_out[lax.clamp(0, at, size_x - 1)] = density[:size_y, :size_z]

        return 0

    lax.fori_loop(0, size_x + 6, material, 0)

    first_modes = plane_modes([field[comp + 1, 2] for comp in range(3)], rows, lanes)
    for number, key in enumerate(KEYS):
        held[number] = first_modes[key]
        carry[number] = jnp.zeros((rows, lanes), f32)

    def operate(step, _):
        old = {key: held[number] for number, key in enumerate(KEYS)}
        new = plane_modes([field[comp + 1, step + 3] for comp in range(3)], rows, lanes)
        for number, key in enumerate(KEYS):
            held[number] = new[key]
        modes = element_modes(old, new)
        stiff = moduli[step]
        forces = modal_product(modal, modes)
        at_node = {}
        for number, key in enumerate(KEYS):
            even, odd = forces[key_row(0, key)], forces[key_row(1, key)]
            odd = odd * stiff
            even = jnp.zeros_like(odd) if even is None else even * stiff
            at_node[key] = carry[number] + (even - odd)
            carry[number] = even + odd
        mask = masks[0] * inside_x(step - 3)
        for comp in range(3):
            along = []
            for mode_z in range(2):
                even, odd = at_node[(comp, 0, mode_z)], at_node[(comp, 1, mode_z)]
                along.append((even - odd) + roll(even + odd, 1, 0))
            total = (along[0] - along[1]) + roll(along[0] + along[1], 1, 1)
            applied[comp, step] = (total + spring_rate * field[comp + 1, step + 2]) * mask
        return 0

    lax.fori_loop(0, size_x + 6, operate, 0)

    first_modes = plane_modes([applied[comp, 3] for comp in range(3)], size_y, size_z)
    for number, key in enumerate(KEYS):
        small_held[number] = first_modes[key]

    def products(step, sums):
        rr, rs, ss, es = sums
        for comp in range(3):
            res = load[comp, step]
            app = applied[comp, step + 3, :size_y, :size_z]
            rr, rs, ss = rr + res * res, rs + res * app, ss + app * app
        old = {key: small_held[number] for number, key in enumerate(KEYS)}
        new = plane_modes([applied[comp, step + 4] for comp in range(3)], size_y, size_z)
        for number, key in enumerate(KEYS):
            small_held[number] = new[key]
        energy = modal_energy(modal, element_modes(old, new))
        return rr, rs, ss, es + energy * moduli[step + 3, :size_y, :size_z]

    nothing = jnp.zeros((size_y, size_z), f32)
    sums = lax.fori_loop(0, size_x, products, (nothing,) * 4)
    row8 = lax.broadcasted_iota(jnp.int32, (8, LANES), 0)
    tile = jnp.zeros((8, LANES), f32)
    for number, value in enumerate(sums):
        line = jnp.sum(value, axis=0, keepdims=True)
        line = sum(line[:, at : at + LANES] for at in range(0, size_z, LANES))
        tile = jnp.where(row8 == number, line, tile)

    def all_sum(slots, partner, count, send, recv):
        copies = [
            pltpu.make_async_remote_copy(
                src_ref=slots.at[0], dst_ref=slots.at[step], send_sem=send.at[step],
                recv_sem=recv.at[step], device_id=partner(step), device_id_type=MESH,
            )
            for step in range(1, count)
        ]
        for copy in copies:
            copy.start()
        total = slots[0]
        for step, copy in enumerate(copies):
            copy.wait_recv()
            total = total + slots[step + 1]
        for copy in copies:
            copy.wait_send()
        return total

    part_z[0] = tile
    part_xy[0] = all_sum(part_z, z_partner, count_z, z_send, z_recv)
    total = all_sum(part_xy, xy_partner, count_x * count_y, xy_send, xy_recv)
    total = jnp.sum(total, axis=1, keepdims=True)
    rr, rs, ss, es = (total[number : number + 1] for number in range(4))
    st = es + spring_rate * ss
    step_first = rr / rs
    rr_next = step_first * step_first * ss - rr
    product = rs - 2.0 * step_first * ss + step_first * step_first * st
    ratio = rr_next / rr
    step_second = rr_next / (product - ratio * rr_next / step_first)
    by_load = step_first + step_second * (1.0 + ratio)
    by_applied = -step_first * step_second

    def displaced(comp, plane):
        return by_load * field[comp + 1, plane + 2] + by_applied * applied[comp, plane]

    first_modes = plane_modes([displaced(comp, 1) for comp in range(3)], rows, lanes)
    for number, key in enumerate(KEYS):
        held[number] = first_modes[key]

    def energies(step, _):
        old = {key: held[number] for number, key in enumerate(KEYS)}
        values = [displaced(comp, step + 2) for comp in range(3)]
        at = step - 1

        @pl.when((at >= 0) & (at < size_x))
        def _():
            for comp in range(3):
                disp_out[comp, lax.clamp(0, at, size_x - 1)] = values[comp][:size_y, :size_z]

        new = plane_modes(values, rows, lanes)
        for number, key in enumerate(KEYS):
            held[number] = new[key]
        push = modal_energy(modal, element_modes(old, new)) * factor[step + 1]
        for far_x, value in enumerate(cone_planes(table, push, size_y, size_z)):
            pushed[far_x, step] = value
        return 0

    lax.fori_loop(0, size_x + 4, energies, 0)

    def finish(plane, _):
        sens_out[plane] = gathered(pushed, plane + 2)
        return 0

    lax.fori_loop(0, size_x, finish, 0)


def solution(mesh):
    counts = tuple(mesh.shape[name] for name in ("gx", "gy", "gz"))
    placed = (P(None, "gx", "gy", "gz"), P("gx", "gy", "gz"), P())

    def body(load_field, design, solid_map):
        size_x, size_y, size_z = design.shape
        rows, lanes = size_y + 2 * PAD, size_z + LANES
        planes = size_x + 2 * HALO
        tiles = -(-planes * PAD // LANES)
        f32 = jnp.float32
        vmem = pl.BlockSpec(memory_space=pltpu.VMEM)
        pairs = counts[0] * counts[1]
        dma = pltpu.SemaphoreType.DMA

        def run(*refs):
            kernel(counts, *refs)

        return pl.pallas_call(
            run,
            out_shape=(
                jax.ShapeDtypeStruct(load_field.shape, f32),
                jax.ShapeDtypeStruct(design.shape, f32),
                jax.ShapeDtypeStruct(design.shape, f32),
            ),
            in_specs=[vmem, vmem, pl.BlockSpec(memory_space=pltpu.SMEM)],
            out_specs=(vmem, vmem, vmem),
            scratch_shapes=[
                pltpu.VMEM((4, planes, rows, lanes), f32),
                pltpu.VMEM((3, size_x + 6, rows, lanes), f32),
                pltpu.VMEM((size_x + 6, rows, lanes), f32),
                pltpu.VMEM((size_x + 6, rows, lanes), f32),
                pltpu.VMEM((size_x // BRICK + 2, rows, lanes), f32),
                pltpu.VMEM((3, planes, rows, lanes), f32),
                pltpu.VMEM((3, size_x + 4, size_y, size_z), f32),
                pltpu.VMEM((12, rows, lanes), f32),
                pltpu.VMEM((12, rows, lanes), f32),
                pltpu.VMEM((12, size_y, size_z), f32),
                pltpu.VMEM((2, 4, tiles, rows, LANES), f32),
                pltpu.VMEM((2, 4, tiles, rows, LANES), f32),
                pltpu.VMEM((4, rows, lanes), f32),
                pltpu.VMEM((counts[2], 8, LANES), f32),
                pltpu.VMEM((pairs, 8, LANES), f32),
                dma((6,)),
                dma((6,)),
                dma((counts[2],)),
                dma((counts[2],)),
                dma((pairs,)),
                dma((pairs,)),
            ],
            compiler_params=pltpu.CompilerParams(
                collective_id=0, has_side_effects=True, vmem_limit_bytes=40 * 2**20
            ),
        )(load_field, design, solid_map)

    return jax.shard_map(
        body,
        mesh=mesh,
        in_specs=placed,
        out_specs=(P(None, "gx", "gy", "gz"), P("gx", "gy", "gz"), P("gx", "gy", "gz")),
        check_vma=False,
    )
```

```python
import itertools
import math

import jax
import jax.numpy as jnp
import numpy as np
from jax import lax
from jax.experimental import pallas as pl
from jax.experimental.pallas import tpu as pltpu
from jax.sharding import PartitionSpec as P

BRICK = 16
HALO = 5
PAD = 8
LANES = 128

young_floor = 0.001
spring_rate = 0.05
sharpness = 8.0
threshold = 0.5
poisson = 0.3
MESH = pl.DeviceIdType.MESH


def element_matrix():
    lame_first = poisson / ((1.0 + poisson) * (1.0 - 2.0 * poisson))
    shear_mod = 1.0 / (2.0 * (1.0 + poisson))
    elastic = np.zeros((6, 6))
    elastic[:3, :3] = lame_first
    for axis_one in range(3):
        elastic[axis_one, axis_one] += 2.0 * shear_mod
        elastic[axis_one + 3, axis_one + 3] = shear_mod
    gauss_point = 1.0 / math.sqrt(3.0)
    stiffness = np.zeros((24, 24))
    for point_x in (-gauss_point, gauss_point):
        for point_y in (-gauss_point, gauss_point):
            for point_z in (-gauss_point, gauss_point):
                strain = np.zeros((6, 24))
                for corner in range(8):
                    sign_a = 2 * (corner // 4) - 1
                    sign_b = 2 * (corner // 2 % 2) - 1
                    sign_c = 2 * (corner % 2) - 1
                    along_x = 0.25 * sign_a * (1 + sign_b * point_y) * (1 + sign_c * point_z)
                    along_y = 0.25 * (1 + sign_a * point_x) * sign_b * (1 + sign_c * point_z)
                    along_z = 0.25 * (1 + sign_a * point_x) * (1 + sign_b * point_y) * sign_c
                    column = 3 * corner
                    strain[0, column] = along_x
                    strain[1, column + 1] = along_y
                    strain[2, column + 2] = along_z
                    strain[3, column + 1] = along_z
                    strain[3, column + 2] = along_y
                    strain[4, column] = along_z
                    strain[4, column + 2] = along_x
                    strain[5, column] = along_y
                    strain[5, column + 1] = along_x
                stiffness += strain.T @ elastic @ strain * 0.125
    return stiffness


def cone_offsets():
    listed = []
    for step_x in range(-2, 3):
        for step_y in range(-2, 3):
            for step_z in range(-2, 3):
                radius = step_x * step_x + step_y * step_y + step_z * step_z
                if radius < 9:
                    listed.append((step_x, step_y, step_z, 3.0 - math.sqrt(radius)))
    return listed


def modal_matrix():
    stiffness = element_matrix()
    change = np.zeros((24, 24))
    for mode in itertools.product((0, 1), repeat=3):
        for corner in itertools.product((0, 1), repeat=3):
            sign = 1.0
            for is_diff, side in zip(mode, corner):
                sign *= (2 * side - 1) if is_diff else 1
            for comp in range(3):
                row = 3 * (4 * mode[0] + 2 * mode[1] + mode[2]) + comp
                change[row, 3 * (4 * corner[0] + 2 * corner[1] + corner[2]) + comp] = sign
    modal = change @ stiffness @ change.T / 64.0
    modal[np.abs(modal) < 1e-10] = 0.0
    return modal


def cone_table():
    table = {}
    for step_x, step_y, step_z, weight in cone_offsets():
        if min(step_x, step_y, step_z) >= 0:
            table[(step_x, step_y, step_z)] = weight
    return table


MODES = tuple(itertools.product((0, 1), repeat=2))


def roll(value, shift):
    return pltpu.roll(value, shift % value.shape[1], 1)


def roll_rows(value, shift, height):
    main, edge = value[:-PAD], value[-PAD:]
    group = LANES * PAD // main.shape[0]
    main = pltpu.roll(main, shift % main.shape[0], 0)[:height]
    edge = pltpu.roll(edge, shift % PAD, 0)
    row = lax.broadcasted_iota(jnp.int32, edge.shape, 0)
    moved = row < shift if shift > 0 else row >= PAD + shift
    other = roll(edge, group if shift > 0 else -group)
    return jnp.concatenate([main, jnp.where(moved, other, edge)], 0)


def shorten(value, height):
    if value.shape[0] == height + PAD:
        return value
    return jnp.concatenate([value[:height], value[-PAD:]], 0)


def patched(value, count):
    edge = value[-PAD:]
    height = value.shape[0] - PAD
    group = LANES // count
    lane = lax.broadcasted_iota(jnp.int32, edge.shape, 1)
    out = []
    for tile in range(height // PAD):
        low = roll(edge, -(tile * group + PAD))
        high = roll(edge, LANES - 3 * PAD - tile * group)
        mine = jnp.where(lane < 2, low, value[tile * PAD : (tile + 1) * PAD])
        out.append(jnp.where(lane >= LANES - 3, high, mine))
    return jnp.concatenate(out, 0)


def plane_modes(values, height):
    out = {}
    for comp, value in enumerate(values):
        ahead = roll(value, -1)
        for mode_z, part in enumerate((value + ahead, ahead - value)):
            above = roll_rows(part, -1, height)
            part = shorten(part, height)
            out[(comp, 0, mode_z)] = part + above
            out[(comp, 1, mode_z)] = above - part
    return out


def modal_product(modal, modes):
    out = {}
    for row in range(24):
        total = None
        for col in range(24):
            if modal[row, col] != 0.0:
                term = modes[col] * float(modal[row, col])
                total = term if total is None else total + term
        out[row] = total
    return out


def key_row(mode_x, key):
    comp, mode_y, mode_z = key
    return 3 * (4 * mode_x + 2 * mode_y + mode_z) + comp


KEYS = tuple((comp, my, mz) for comp in range(3) for my, mz in MODES)


def element_modes(old, new):
    modes = {}
    for key in KEYS:
        modes[key_row(0, key)] = old[key] + new[key]
        modes[key_row(1, key)] = new[key] - old[key]
    return modes


def modal_energy(modal, modes):
    forces = modal_product(modal, modes)
    total = None
    for row in range(24):
        if forces[row] is not None:
            term = forces[row] * modes[row]
            total = term if total is None else total + term
    return total


def cone_planes(table, value, height):
    along_z = (
        value,
        roll(value, 1) + roll(value, -1),
        roll(value, 2) + roll(value, -2),
    )
    sums = [None, None, None]
    for far_z, part in enumerate(along_z):
        along_y = (
            shorten(part, height),
            roll_rows(part, 1, height) + roll_rows(part, -1, height),
            roll_rows(part, 2, height) + roll_rows(part, -2, height),
        )
        for far_x in range(3):
            for far_y in range(3):
                weight = table.get((far_x, far_y, far_z))
                if weight is not None:
                    term = along_y[far_y] * weight
                    sums[far_x] = term if sums[far_x] is None else sums[far_x] + term
    return sums


def kernel(
    counts,
    load,
    design,
    solid,
    disp_out,
    sens_out,
    dens_out,
    field,
    applied,
    moduli,
    factor,
    flags,
    cone,
    pushed,
    held,
    carry,
    small_held,
    packed,
    arrived,
    masks,
    part_z,
    part_xy,
    face_send,
    face_recv,
    z_send,
    z_recv,
    xy_send,
    xy_recv,
    copy_sem,
):
    count_x, count_y, count_z = counts
    size_x, size_y, size_z = design.shape
    rows = size_y + 2 * PAD
    full, lanes = rows + PAD, size_z
    count_t = rows // PAD
    group = LANES // count_t
    planes = size_x + 2 * HALO
    first, last = lax.axis_index("gx") == 0, lax.axis_index("gx") == count_x - 1
    ix, iy, iz = lax.axis_index("gx"), lax.axis_index("gy"), lax.axis_index("gz")
    modal = modal_matrix()
    table = cone_table()
    f32 = jnp.float32

    def z_partner(step):
        return (ix, iy, lax.rem(iz + step, count_z))

    def xy_partner(step):
        spot = lax.rem(ix * count_y + iy + step, count_x * count_y)
        return (spot // count_y, lax.rem(spot, count_y), iz)

    inner = pl.ds(HALO, size_x)
    bring = [pltpu.make_async_copy(design, field.at[0, inner, pl.ds(0, size_y)], copy_sem.at[0])]
    for comp in range(3):
        bring.append(
            pltpu.make_async_copy(
                load.at[comp], field.at[comp + 1, inner, pl.ds(0, size_y)], copy_sem.at[comp + 1]
            )
        )
    for copy in bring:
        copy.start()

    for index in range(4):

        def clear(plane, _):
            field[index, plane + HALO, size_y:rows] = jnp.zeros((rows - size_y, lanes), f32)
            return 0

        lax.fori_loop(0, size_x, clear, 0)
        for plane in range(HALO):
            field[index, plane, :rows] = jnp.zeros((rows, lanes), f32)
            field[index, plane + HALO + size_x, :rows] = jnp.zeros((rows, lanes), f32)

    @pl.when(iz == 0)
    def _():
        arrived[1] = jnp.zeros(arrived.shape[1:], f32)

    @pl.when(iz == count_z - 1)
    def _():
        arrived[0] = jnp.zeros(arrived.shape[1:], f32)

    barrier = pltpu.get_barrier_semaphore()
    for step in range(1, count_z):
        pl.semaphore_signal(barrier, inc=1, device_id=z_partner(step), device_id_type=MESH)
    for step in range(1, count_x * count_y):
        pl.semaphore_signal(barrier, inc=1, device_id=xy_partner(step), device_id_type=MESH)
    pl.semaphore_wait(barrier, count_z - 1 + count_x * count_y - 1)
    for copy in bring:
        copy.wait()

    def exchange(slot, down, up, down_id, up_id, has_down, has_up):
        to_down = pltpu.make_async_remote_copy(
            src_ref=down[0], dst_ref=down[1], send_sem=face_send.at[slot],
            recv_sem=face_recv.at[slot], device_id=down_id, device_id_type=MESH,
        )
        to_up = pltpu.make_async_remote_copy(
            src_ref=up[0], dst_ref=up[1], send_sem=face_send.at[slot + 1],
            recv_sem=face_recv.at[slot + 1], device_id=up_id, device_id_type=MESH,
        )

        @pl.when(has_down)
        def _():
            to_down.start()

        @pl.when(has_up)
        def _():
            to_up.start()

        @pl.when(has_up)
        def _():
            to_down.wait_recv()
            to_up.wait_send()

        @pl.when(has_down)
        def _():
            to_up.wait_recv()
            to_down.wait_send()

    main = pl.ds(0, size_z)
    exchange(
        0,
        (field.at[:, inner, pl.ds(0, PAD), main], field.at[:, inner, pl.ds(size_y, PAD), main]),
        (
            field.at[:, inner, pl.ds(size_y - PAD, PAD), main],
            field.at[:, inner, pl.ds(size_y + PAD, PAD), main],
        ),
        (ix, lax.max(iy - 1, 0), iz),
        (ix, lax.min(iy + 1, count_y - 1), iz),
        iy > 0,
        iy < count_y - 1,
    )
    every = pl.ds(0, rows)
    exchange(
        2,
        (
            field.at[:, pl.ds(HALO, HALO), every, main],
            field.at[:, pl.ds(HALO + size_x, HALO), every, main],
        ),
        (field.at[:, pl.ds(size_x, HALO), every, main], field.at[:, pl.ds(0, HALO), every, main]),
        (lax.max(ix - 1, 0), iy, iz),
        (lax.min(ix + 1, count_x - 1), iy, iz),
        ix > 0,
        ix < count_x - 1,
    )

    lane_of = lax.broadcasted_iota(jnp.int32, (PAD, LANES), 1)
    in_group = lax.rem(lane_of, group)

    def pack(plane, _):
        for index in range(4):
            out = jnp.zeros((PAD, LANES), f32)
            for tile in range(count_t):
                at = tile * group
                mine = field[index, plane, tile * PAD : (tile + 1) * PAD]
                here = (lane_of >= at + PAD) & (lane_of < at + 2 * PAD)
                out = jnp.where(here, roll(mine, at + PAD), out)
                here = (lane_of >= at + 2 * PAD) & (lane_of < at + 3 * PAD)
                out = jnp.where(here, roll(mine, at + 3 * PAD), out)
            packed[index, plane] = out
        return 0

    lax.fori_loop(0, planes, pack, 0)
    exchange(
        4,
        (packed, arrived.at[0]),
        (packed, arrived.at[1]),
        (ix, iy, lax.max(iz - 1, 0)),
        (ix, iy, lax.min(iz + 1, count_z - 1)),
        iz > 0,
        iz < count_z - 1,
    )

    def unpack(plane, _):
        for index in range(4):
            below = roll(arrived[1, index, plane], -2 * PAD)
            above = roll(arrived[0, index, plane], 2 * PAD)
            value = jnp.where(in_group < PAD, below, packed[index, plane])
            field[index, plane, rows:] = jnp.where(in_group >= 3 * PAD, above, value)
        return 0

    lax.fori_loop(0, planes, unpack, 0)

    row_at = lax.broadcasted_iota(jnp.int32, (rows, lanes), 0)
    lane_at = lax.broadcasted_iota(jnp.int32, (rows, lanes), 1)
    edge_row = lax.broadcasted_iota(jnp.int32, (PAD, lanes), 0) + lane_of // group * PAD
    edge_lane = jnp.where(in_group < 2 * PAD, in_group - PAD, in_group + size_z - 3 * PAD)
    row_at = jnp.concatenate([row_at, edge_row], 0)
    lane_at = jnp.concatenate([lane_at, edge_lane], 0) + iz * size_z
    row_at = jnp.where(row_at < size_y + PAD, row_at, row_at - rows) + iy * size_y
    inside_yz = (
        (row_at >= 0) & (row_at < size_y * count_y) & (lane_at >= 0) & (lane_at < size_z * count_z)
    )
    masks[0] = jnp.where(inside_yz, 1.0, 0.0).astype(f32)
    for far_x, value in enumerate(cone_planes(table, masks[0], rows)):
        masks[1 + far_x, :rows] = patched(value, count_t)
        masks[1 + far_x, rows:] = value[rows:]

    def inside_x(plane):
        where = plane + ix * size_x
        return jnp.where((where >= 0) & (where < size_x * count_x), 1.0, 0.0).astype(f32)

    bricks_x, bricks_y, bricks_z = size_x // BRICK, size_y // BRICK, size_z // BRICK

    def brick(bx, by, bz):
        gx, gy, gz = ix * bricks_x + bx, iy * bricks_y + by, iz * bricks_z + bz
        top_x, top_y, top_z = bricks_x * count_x, bricks_y * count_y, bricks_z * count_z
        good = (gx >= 0) & (gx < top_x) & (gy >= 0) & (gy < top_y) & (gz >= 0) & (gz < top_z)
        value = solid[
            lax.clamp(0, gx, top_x - 1), lax.clamp(0, gy, top_y - 1), lax.clamp(0, gz, top_z - 1)
        ]
        return value.astype(f32) * jnp.where(good, 1.0, 0.0).astype(f32)

    for bx in range(-1, bricks_x + 1):
        edge = jnp.zeros((PAD, lanes), f32)
        for by in range(-1, bricks_y + 1):
            line = jnp.zeros((PAD, lanes), f32)
            for bz in range(bricks_z):
                here = (lane_of >= bz * BRICK) & (lane_of < (bz + 1) * BRICK)
                line = jnp.where(here, brick(bx, by, bz), line)
            if by < 0:
                spots = [size_y + PAD]
            elif by == bricks_y:
                spots = [size_y]
            else:
                spots = range(by * BRICK, (by + 1) * BRICK, PAD)
            around = jnp.zeros((PAD, lanes), f32)
            for part, bz in enumerate((-1, 0, bricks_z - 1, bricks_z)):
                around = jnp.where(in_group >= part * PAD, brick(bx, by, bz), around)
            for spot in spots:
                flags[bx + 1, spot : spot + PAD, :] = line
                edge = jnp.where(lane_of // group == spot // PAD, around, edge)
        flags[bx + 1, rows:, :] = edge

    def filter_plane(plane, _):
        for far_x, value in enumerate(cone_planes(table, field[0, plane], rows)):
            cone[far_x, plane] = value
        return 0

    lax.fori_loop(jnp.where(first, 3, 0), jnp.where(last, planes - 3, planes), filter_plane, 0)
    lift = math.tanh(sharpness * threshold)
    scale = lift + math.tanh(sharpness * (1.0 - threshold))

    def gathered(source, plane):
        return (
            source[0, plane]
            + (source[1, plane - 1] + source[1, plane + 1])
            + (source[2, plane - 2] + source[2, plane + 2])
        )

    def material(step, _):
        at = step - 3
        plane = step + 2
        weight = inside_x(at) * masks[1]
        weight = weight + (inside_x(at - 1) + inside_x(at + 1)) * masks[2]
        weight = weight + (inside_x(at - 2) + inside_x(at + 2)) * masks[3]
        weight = 1.0 / jnp.maximum(weight, 1.0)
        smoothed = gathered(cone, plane)
        smoothed = jnp.concatenate([patched(smoothed, count_t), smoothed[rows:]], 0)
        tanh_shift = jnp.tanh(sharpness * (smoothed * weight - threshold))
        density = (lift + tanh_shift) * (1.0 / scale)
        flag = flags[(at + BRICK) // BRICK]
        squared = density * density
        moduli[step] = (young_floor + (1.0 - young_floor) * (squared * density)) * flag
        slope = (1.0 - tanh_shift * tanh_shift) * weight
        factor[step] = (
            (-3.0 * (1.0 - young_floor) * sharpness / scale) * (squared * flag) * slope
        )

        @pl.when((at >= 0) & (at < size_x))
        def _():
            dens_out[lax.clamp(0, at, size_x - 1)] = density[:size_y]

        return 0

    begin, end = jnp.where(first, 3, 0), jnp.where(last, size_x + 3, size_x + 6)
    lax.fori_loop(begin, end, material, 0)

    first_modes = plane_modes([field[comp + 1, begin + 2] for comp in range(3)], rows)
    for number, key in enumerate(KEYS):
        held[number] = first_modes[key]
        carry[number] = jnp.zeros((full, lanes), f32)

    def operate(step, _):
        old = {key: held[number] for number, key in enumerate(KEYS)}
        new = plane_modes([field[comp + 1, step + 3] for comp in range(3)], rows)
        for number, key in enumerate(KEYS):
            held[number] = new[key]
        modes = element_modes(old, new)
        stiff = moduli[step]
        forces = modal_product(modal, modes)
        at_node = {}
        for number, key in enumerate(KEYS):
            even, odd = forces[key_row(0, key)], forces[key_row(1, key)]
            odd = odd * stiff
            even = jnp.zeros_like(odd) if even is None else even * stiff
            at_node[key] = carry[number] + (even - odd)
            carry[number] = even + odd
        mask = masks[0] * inside_x(step - 3)
        for comp in range(3):
            along = []
            for mode_z in range(2):
                even, odd = at_node[(comp, 0, mode_z)], at_node[(comp, 1, mode_z)]
                along.append((even - odd) + roll_rows(even + odd, 1, rows))
            total = (along[0] - along[1]) + roll(along[0] + along[1], 1)
            total = (total + spring_rate * field[comp + 1, step + 2]) * mask
            applied[comp, step, :rows] = patched(total, count_t)
            applied[comp, step, rows:] = total[rows:]
        return 0

    lax.fori_loop(begin, end, operate, 0)

    @pl.when(last)
    def _():
        for comp in range(3):
            applied[comp, size_x + 3] = jnp.zeros((full, lanes), f32)


    first_modes = plane_modes([applied[comp, 3] for comp in range(3)], size_y)
    for number, key in enumerate(KEYS):
        small_held[number] = first_modes[key]

    def products(step, sums):
        rr, rs, ss, es = sums
        for comp in range(3):
            res = field[comp + 1, step + HALO, :size_y]
            app = applied[comp, step + 3, :size_y]
            rr, rs, ss = rr + res * res, rs + res * app, ss + app * app
        old = {key: small_held[number] for number, key in enumerate(KEYS)}
        new = plane_modes([applied[comp, step + 4] for comp in range(3)], size_y)
        for number, key in enumerate(KEYS):
            small_held[number] = new[key]
        energy = modal_energy(modal, element_modes(old, new))
        return rr, rs, ss, es + energy * shorten(moduli[step + 3], size_y)

    nothing = jnp.zeros((size_y, size_z), f32)
    most = jnp.zeros((size_y + PAD, size_z), f32)
    sums = list(lax.fori_loop(0, size_x, products, (nothing, nothing, nothing, most)))
    lane_main = lax.broadcasted_iota(jnp.int32, (size_y, lanes), 1)
    strain = jnp.where(lane_main < size_z - 1, sums[3][:size_y], 0.0)
    ends = (in_group == 3 * PAD - 1) & (lane_of < size_y // PAD * group)
    sums[3] = jnp.concatenate([strain, jnp.where(ends, sums[3][size_y:], 0.0)], 0)
    row8 = lax.broadcasted_iota(jnp.int32, (8, LANES), 0)
    tile = jnp.zeros((8, LANES), f32)
    for number, value in enumerate(sums):
        line = jnp.sum(value, axis=0, keepdims=True)
        tile = jnp.where(row8 == number, line, tile)

    def all_sum(slots, partner, count, send, recv):
        copies = [
            pltpu.make_async_remote_copy(
                src_ref=slots.at[0], dst_ref=slots.at[step], send_sem=send.at[step],
                recv_sem=recv.at[step], device_id=partner(step), device_id_type=MESH,
            )
            for step in range(1, count)
        ]
        for copy in copies:
            copy.start()
        total = slots[0]
        for step, copy in enumerate(copies):
            copy.wait_recv()
            total = total + slots[step + 1]
        for copy in copies:
            copy.wait_send()
        return total

    part_z[0] = tile
    part_xy[0] = all_sum(part_z, z_partner, count_z, z_send, z_recv)
    total = all_sum(part_xy, xy_partner, count_x * count_y, xy_send, xy_recv)
    total = jnp.sum(total, axis=1, keepdims=True)
    rr, rs, ss, es = (total[number : number + 1] for number in range(4))
    st = es + spring_rate * ss
    step_first = rr / rs
    rr_next = step_first * step_first * ss - rr
    product = rs - 2.0 * step_first * ss + step_first * step_first * st
    ratio = rr_next / rr
    step_second = rr_next / (product - ratio * rr_next / step_first)
    by_load = step_first + step_second * (1.0 + ratio)
    by_applied = -step_first * step_second

    def displaced(comp, plane):
        return by_load * field[comp + 1, plane + 2] + by_applied * applied[comp, plane]

    begin, end = jnp.where(first, 2, 0), jnp.where(last, size_x + 2, size_x + 4)
    for far_x in range(3):
        for side, spot in ((first, 0), (last, size_x + 2)):

            @pl.when(side)
            def _():
                pushed[far_x, spot : spot + 2] = jnp.zeros((2, size_y + PAD, size_z), f32)

    first_modes = plane_modes([displaced(comp, begin + 1) for comp in range(3)], rows)
    for number, key in enumerate(KEYS):
        held[number] = first_modes[key]

    def energies(step, _):
        old = {key: held[number] for number, key in enumerate(KEYS)}
        values = [displaced(comp, step + 2) for comp in range(3)]
        new = plane_modes(values, rows)
        for number, key in enumerate(KEYS):
            held[number] = new[key]
        push = modal_energy(modal, element_modes(old, new)) * factor[step + 1]
        for far_x, value in enumerate(cone_planes(table, push, size_y)):
            pushed[far_x, step] = value
        return 0

    lax.fori_loop(begin, end, energies, 0)

    def finish(plane, _):
        sens_out[plane] = patched(gathered(pushed, plane + 2), count_t)
        for comp in range(3):
            disp_out[comp, plane] = displaced(comp, plane + 3)[:size_y]
        return 0

    lax.fori_loop(0, size_x, finish, 0)


def solution(mesh):
    counts = tuple(mesh.shape[name] for name in ("gx", "gy", "gz"))
    placed = (P(None, "gx", "gy", "gz"), P("gx", "gy", "gz"), P())

    def body(load_field, design, solid_map):
        size_x, size_y, size_z = design.shape
        rows = size_y + 2 * PAD
        full, lanes = rows + PAD, size_z
        planes = size_x + 2 * HALO
        f32 = jnp.float32
        vmem = pl.BlockSpec(memory_space=pltpu.VMEM)
        anywhere = pl.BlockSpec(memory_space=pl.ANY)
        pairs = counts[0] * counts[1]
        dma = pltpu.SemaphoreType.DMA

        def run(*refs):
            kernel(counts, *refs)

        return pl.pallas_call(
            run,
            out_shape=(
                jax.ShapeDtypeStruct(load_field.shape, f32),
                jax.ShapeDtypeStruct(design.shape, f32),
                jax.ShapeDtypeStruct(design.shape, f32),
            ),
            in_specs=[anywhere, anywhere, pl.BlockSpec(memory_space=pltpu.SMEM)],
            out_specs=(vmem, vmem, vmem),
            scratch_shapes=[
                pltpu.VMEM((4, planes, full, lanes), f32),
                pltpu.VMEM((3, size_x + 6, full, lanes), f32),
                pltpu.VMEM((size_x + 6, full, lanes), f32),
                pltpu.VMEM((size_x + 6, full, lanes), f32),
                pltpu.VMEM((size_x // BRICK + 2, full, lanes), f32),
                pltpu.VMEM((3, planes, full, lanes), f32),
                pltpu.VMEM((3, size_x + 4, size_y + PAD, size_z), f32),
                pltpu.VMEM((12, full, lanes), f32),
                pltpu.VMEM((12, full, lanes), f32),
                pltpu.VMEM((12, size_y + PAD, size_z), f32),
                pltpu.VMEM((4, planes, PAD, LANES), f32),
                pltpu.VMEM((2, 4, planes, PAD, LANES), f32),
                pltpu.VMEM((4, full, lanes), f32),
                pltpu.VMEM((counts[2], 8, LANES), f32),
                pltpu.VMEM((pairs, 8, LANES), f32),
                dma((6,)),
                dma((6,)),
                dma((counts[2],)),
                dma((counts[2],)),
                dma((pairs,)),
                dma((pairs,)),
                dma((4,)),
            ],
            compiler_params=pltpu.CompilerParams(
                collective_id=0, has_side_effects=True, vmem_limit_bytes=40 * 2**20
            ),
        )(load_field, design, solid_map)

    return jax.shard_map(
        body,
        mesh=mesh,
        in_specs=placed,
        out_specs=(P(None, "gx", "gy", "gz"), P("gx", "gy", "gz"), P("gx", "gy", "gz")),
        check_vma=False,
    )
```

```python
import itertools
import math

import jax
import jax.numpy as jnp
import numpy as np
from jax import lax
from jax.experimental import pallas as pl
from jax.experimental.pallas import tpu as pltpu
from jax.sharding import PartitionSpec as P

BRICK = 16
HALO = 5
PAD = 8
LANES = 128

young_floor = 0.001
spring_rate = 0.05
sharpness = 8.0
threshold = 0.5
poisson = 0.3
MESH = pl.DeviceIdType.MESH


def element_matrix():
    lame_first = poisson / ((1.0 + poisson) * (1.0 - 2.0 * poisson))
    shear_mod = 1.0 / (2.0 * (1.0 + poisson))
    elastic = np.zeros((6, 6))
    elastic[:3, :3] = lame_first
    for axis_one in range(3):
        elastic[axis_one, axis_one] += 2.0 * shear_mod
        elastic[axis_one + 3, axis_one + 3] = shear_mod
    gauss_point = 1.0 / math.sqrt(3.0)
    stiffness = np.zeros((24, 24))
    for point_x in (-gauss_point, gauss_point):
        for point_y in (-gauss_point, gauss_point):
            for point_z in (-gauss_point, gauss_point):
                strain = np.zeros((6, 24))
                for corner in range(8):
                    sign_a = 2 * (corner // 4) - 1
                    sign_b = 2 * (corner // 2 % 2) - 1
                    sign_c = 2 * (corner % 2) - 1
                    along_x = 0.25 * sign_a * (1 + sign_b * point_y) * (1 + sign_c * point_z)
                    along_y = 0.25 * (1 + sign_a * point_x) * sign_b * (1 + sign_c * point_z)
                    along_z = 0.25 * (1 + sign_a * point_x) * (1 + sign_b * point_y) * sign_c
                    column = 3 * corner
                    strain[0, column] = along_x
                    strain[1, column + 1] = along_y
                    strain[2, column + 2] = along_z
                    strain[3, column + 1] = along_z
                    strain[3, column + 2] = along_y
                    strain[4, column] = along_z
                    strain[4, column + 2] = along_x
                    strain[5, column] = along_y
                    strain[5, column + 1] = along_x
                stiffness += strain.T @ elastic @ strain * 0.125
    return stiffness


def cone_offsets():
    listed = []
    for step_x in range(-2, 3):
        for step_y in range(-2, 3):
            for step_z in range(-2, 3):
                radius = step_x * step_x + step_y * step_y + step_z * step_z
                if radius < 9:
                    listed.append((step_x, step_y, step_z, 3.0 - math.sqrt(radius)))
    return listed


def modal_matrix():
    stiffness = element_matrix()
    change = np.zeros((24, 24))
    for mode in itertools.product((0, 1), repeat=3):
        for corner in itertools.product((0, 1), repeat=3):
            sign = 1.0
            for is_diff, side in zip(mode, corner):
                sign *= (2 * side - 1) if is_diff else 1
            for comp in range(3):
                row = 3 * (4 * mode[0] + 2 * mode[1] + mode[2]) + comp
                change[row, 3 * (4 * corner[0] + 2 * corner[1] + corner[2]) + comp] = sign
    modal = change @ stiffness @ change.T / 64.0
    modal[np.abs(modal) < 1e-10] = 0.0
    return modal


def cone_table():
    table = {}
    for step_x, step_y, step_z, weight in cone_offsets():
        if min(step_x, step_y, step_z) >= 0:
            table[(step_x, step_y, step_z)] = weight
    return table


MODES = tuple(itertools.product((0, 1), repeat=2))


def roll(value, shift):
    return pltpu.roll(value, shift % value.shape[1], 1)


def roll_rows(value, shift, height):
    main, edge = value[:-PAD], value[-PAD:]
    group = LANES * PAD // main.shape[0]
    main = pltpu.roll(main, shift % main.shape[0], 0)[:height]
    edge = pltpu.roll(edge, shift % PAD, 0)
    row = lax.broadcasted_iota(jnp.int32, edge.shape, 0)
    moved = row < shift if shift > 0 else row >= PAD + shift
    other = roll(edge, group if shift > 0 else -group)
    return jnp.concatenate([main, jnp.where(moved, other, edge)], 0)


def shorten(value, height):
    if value.shape[0] == height + PAD:
        return value
    return jnp.concatenate([value[:height], value[-PAD:]], 0)


def patched(value, count):
    edge = value[-PAD:]
    height = value.shape[0] - PAD
    group = LANES // count
    lane = lax.broadcasted_iota(jnp.int32, edge.shape, 1)
    out = []
    for tile in range(height // PAD):
        low = roll(edge, -(tile * group + PAD))
        high = roll(edge, LANES - 3 * PAD - tile * group)
        mine = jnp.where(lane < 2, low, value[tile * PAD : (tile + 1) * PAD])
        out.append(jnp.where(lane >= LANES - 3, high, mine))
    return jnp.concatenate(out, 0)


def plane_modes(values, height):
    out = {}
    for comp, value in enumerate(values):
        ahead = roll(value, -1)
        for mode_z, part in enumerate((value + ahead, ahead - value)):
            above = roll_rows(part, -1, height)
            part = shorten(part, height)
            out[(comp, 0, mode_z)] = part + above
            out[(comp, 1, mode_z)] = above - part
    return out


def modal_product(modal, modes):
    out = {}
    for row in range(24):
        total = None
        for col in range(24):
            if modal[row, col] != 0.0:
                term = modes[col] * float(modal[row, col])
                total = term if total is None else total + term
        out[row] = total
    return out


def key_row(mode_x, key):
    comp, mode_y, mode_z = key
    return 3 * (4 * mode_x + 2 * mode_y + mode_z) + comp


KEYS = tuple((comp, my, mz) for comp in range(3) for my, mz in MODES)


def element_modes(old, new):
    modes = {}
    for key in KEYS:
        modes[key_row(0, key)] = old[key] + new[key]
        modes[key_row(1, key)] = new[key] - old[key]
    return modes


def modal_energy(modal, modes):
    forces = modal_product(modal, modes)
    total = None
    for row in range(24):
        if forces[row] is not None:
            term = forces[row] * modes[row]
            total = term if total is None else total + term
    return total


def cone_planes(table, value, height):
    along_z = (
        value,
        roll(value, 1) + roll(value, -1),
        roll(value, 2) + roll(value, -2),
    )
    sums = [None, None, None]
    for far_z, part in enumerate(along_z):
        along_y = (
            shorten(part, height),
            roll_rows(part, 1, height) + roll_rows(part, -1, height),
            roll_rows(part, 2, height) + roll_rows(part, -2, height),
        )
        for far_x in range(3):
            for far_y in range(3):
                weight = table.get((far_x, far_y, far_z))
                if weight is not None:
                    term = along_y[far_y] * weight
                    sums[far_x] = term if sums[far_x] is None else sums[far_x] + term
    return sums


def in_chunks(begin, chunks, size, body):
    def step(number, _):
        body([begin + number * size + at for at in range(size)])
        return 0

    lax.fori_loop(0, chunks, step, 0)


def kernel(
    counts,
    load,
    design,
    solid,
    disp_out,
    sens_out,
    dens_out,
    field,
    applied,
    moduli,
    factor,
    flags,
    cone,
    pushed,
    held,
    carry,
    small_held,
    packed,
    arrived,
    masks,
    part_z,
    part_xy,
    face_send,
    face_recv,
    z_send,
    z_recv,
    xy_send,
    xy_recv,
    copy_sem,
):
    count_x, count_y, count_z = counts
    size_x, size_y, size_z = design.shape
    rows = size_y + 2 * PAD
    full, lanes = rows + PAD, size_z
    count_t = rows // PAD
    group = LANES // count_t
    planes = size_x + 2 * HALO
    first, last = lax.axis_index("gx") == 0, lax.axis_index("gx") == count_x - 1
    ix, iy, iz = lax.axis_index("gx"), lax.axis_index("gy"), lax.axis_index("gz")
    modal = modal_matrix()
    table = cone_table()
    f32 = jnp.float32

    def z_partner(step):
        return (ix, iy, lax.rem(iz + step, count_z))

    def xy_partner(step):
        spot = lax.rem(ix * count_y + iy + step, count_x * count_y)
        return (spot // count_y, lax.rem(spot, count_y), iz)

    inner = pl.ds(HALO, size_x)
    bring = [pltpu.make_async_copy(design, field.at[0, inner, pl.ds(0, size_y)], copy_sem.at[0])]
    for comp in range(3):
        bring.append(
            pltpu.make_async_copy(
                load.at[comp], field.at[comp + 1, inner, pl.ds(0, size_y)], copy_sem.at[comp + 1]
            )
        )
    for copy in bring:
        copy.start()

    for index in range(4):

        def clear(plane, _):
            field[index, plane + HALO, size_y:rows] = jnp.zeros((rows - size_y, lanes), f32)
            return 0

        lax.fori_loop(0, size_x, clear, 0)
        for plane in range(HALO):
            field[index, plane, :rows] = jnp.zeros((rows, lanes), f32)
            field[index, plane + HALO + size_x, :rows] = jnp.zeros((rows, lanes), f32)

    @pl.when(iz == 0)
    def _():
        arrived[1] = jnp.zeros(arrived.shape[1:], f32)

    @pl.when(iz == count_z - 1)
    def _():
        arrived[0] = jnp.zeros(arrived.shape[1:], f32)

    barrier = pltpu.get_barrier_semaphore()
    for step in range(1, count_z):
        pl.semaphore_signal(barrier, inc=1, device_id=z_partner(step), device_id_type=MESH)
    for step in range(1, count_x * count_y):
        pl.semaphore_signal(barrier, inc=1, device_id=xy_partner(step), device_id_type=MESH)
    pl.semaphore_wait(barrier, count_z - 1 + count_x * count_y - 1)
    for copy in bring:
        copy.wait()

    def exchange(slot, down, up, down_id, up_id, has_down, has_up):
        to_down = pltpu.make_async_remote_copy(
            src_ref=down[0], dst_ref=down[1], send_sem=face_send.at[slot],
            recv_sem=face_recv.at[slot], device_id=down_id, device_id_type=MESH,
        )
        to_up = pltpu.make_async_remote_copy(
            src_ref=up[0], dst_ref=up[1], send_sem=face_send.at[slot + 1],
            recv_sem=face_recv.at[slot + 1], device_id=up_id, device_id_type=MESH,
        )

        @pl.when(has_down)
        def _():
            to_down.start()

        @pl.when(has_up)
        def _():
            to_up.start()

        @pl.when(has_up)
        def _():
            to_down.wait_recv()
            to_up.wait_send()

        @pl.when(has_down)
        def _():
            to_up.wait_recv()
            to_down.wait_send()

    main = pl.ds(0, size_z)
    exchange(
        0,
        (field.at[:, inner, pl.ds(0, PAD), main], field.at[:, inner, pl.ds(size_y, PAD), main]),
        (
            field.at[:, inner, pl.ds(size_y - PAD, PAD), main],
            field.at[:, inner, pl.ds(size_y + PAD, PAD), main],
        ),
        (ix, lax.max(iy - 1, 0), iz),
        (ix, lax.min(iy + 1, count_y - 1), iz),
        iy > 0,
        iy < count_y - 1,
    )
    every = pl.ds(0, rows)
    exchange(
        2,
        (
            field.at[:, pl.ds(HALO, HALO), every, main],
            field.at[:, pl.ds(HALO + size_x, HALO), every, main],
        ),
        (field.at[:, pl.ds(size_x, HALO), every, main], field.at[:, pl.ds(0, HALO), every, main]),
        (lax.max(ix - 1, 0), iy, iz),
        (lax.min(ix + 1, count_x - 1), iy, iz),
        ix > 0,
        ix < count_x - 1,
    )

    lane_of = lax.broadcasted_iota(jnp.int32, (PAD, LANES), 1)
    in_group = lax.rem(lane_of, group)

    def pack(chunk):
        for plane, index in itertools.product(chunk, range(4)):
            out = jnp.zeros((PAD, LANES), f32)
            for tile in range(count_t):
                at = tile * group
                mine = field[index, plane, tile * PAD : (tile + 1) * PAD]
                here = (lane_of >= at + PAD) & (lane_of < at + 2 * PAD)
                out = jnp.where(here, roll(mine, at + PAD), out)
                here = (lane_of >= at + 2 * PAD) & (lane_of < at + 3 * PAD)
                out = jnp.where(here, roll(mine, at + 3 * PAD), out)
            packed[index, plane] = out

    in_chunks(0, planes // 2, 2, pack)
    exchange(
        4,
        (packed, arrived.at[0]),
        (packed, arrived.at[1]),
        (ix, iy, lax.max(iz - 1, 0)),
        (ix, iy, lax.min(iz + 1, count_z - 1)),
        iz > 0,
        iz < count_z - 1,
    )

    def unpack(chunk):
        for plane, index in itertools.product(chunk, range(4)):
            below = roll(arrived[1, index, plane], -2 * PAD)
            above = roll(arrived[0, index, plane], 2 * PAD)
            value = jnp.where(in_group < PAD, below, packed[index, plane])
            field[index, plane, rows:] = jnp.where(in_group >= 3 * PAD, above, value)

    in_chunks(0, planes // 2, 2, unpack)

    row_at = lax.broadcasted_iota(jnp.int32, (rows, lanes), 0)
    lane_at = lax.broadcasted_iota(jnp.int32, (rows, lanes), 1)
    edge_row = lax.broadcasted_iota(jnp.int32, (PAD, lanes), 0) + lane_of // group * PAD
    edge_lane = jnp.where(in_group < 2 * PAD, in_group - PAD, in_group + size_z - 3 * PAD)
    row_at = jnp.concatenate([row_at, edge_row], 0)
    lane_at = jnp.concatenate([lane_at, edge_lane], 0) + iz * size_z
    row_at = jnp.where(row_at < size_y + PAD, row_at, row_at - rows) + iy * size_y
    inside_yz = (
        (row_at >= 0) & (row_at < size_y * count_y) & (lane_at >= 0) & (lane_at < size_z * count_z)
    )
    masks[0] = jnp.where(inside_yz, 1.0, 0.0).astype(f32)
    for far_x, value in enumerate(cone_planes(table, masks[0], rows)):
        masks[1 + far_x, :rows] = patched(value, count_t)
        masks[1 + far_x, rows:] = value[rows:]

    def inside_x(plane):
        where = plane + ix * size_x
        return jnp.where((where >= 0) & (where < size_x * count_x), 1.0, 0.0).astype(f32)

    bricks_x, bricks_y, bricks_z = size_x // BRICK, size_y // BRICK, size_z // BRICK

    def brick(bx, by, bz):
        gx, gy, gz = ix * bricks_x + bx, iy * bricks_y + by, iz * bricks_z + bz
        top_x, top_y, top_z = bricks_x * count_x, bricks_y * count_y, bricks_z * count_z
        good = (gx >= 0) & (gx < top_x) & (gy >= 0) & (gy < top_y) & (gz >= 0) & (gz < top_z)
        value = solid[
            lax.clamp(0, gx, top_x - 1), lax.clamp(0, gy, top_y - 1), lax.clamp(0, gz, top_z - 1)
        ]
        return value.astype(f32) * jnp.where(good, 1.0, 0.0).astype(f32)

    for bx in range(-1, bricks_x + 1):
        edge = jnp.zeros((PAD, lanes), f32)
        for by in range(-1, bricks_y + 1):
            line = jnp.zeros((PAD, lanes), f32)
            for bz in range(bricks_z):
                here = (lane_of >= bz * BRICK) & (lane_of < (bz + 1) * BRICK)
                line = jnp.where(here, brick(bx, by, bz), line)
            if by < 0:
                spots = [size_y + PAD]
            elif by == bricks_y:
                spots = [size_y]
            else:
                spots = range(by * BRICK, (by + 1) * BRICK, PAD)
            around = jnp.zeros((PAD, lanes), f32)
            for part, bz in enumerate((-1, 0, bricks_z - 1, bricks_z)):
                around = jnp.where(in_group >= part * PAD, brick(bx, by, bz), around)
            for spot in spots:
                flags[bx + 1, spot : spot + PAD, :] = line
                edge = jnp.where(lane_of // group == spot // PAD, around, edge)
        flags[bx + 1, rows:, :] = edge

    begin = jnp.where(first, 2, 0)
    at_side = first | last

    def filter_planes(chunk):
        for plane in chunk:
            for far_x, value in enumerate(cone_planes(table, field[0, plane], rows)):
                cone[far_x, plane] = value

    in_chunks(begin, jnp.where(at_side, (planes + 1) // 4, (planes + 3) // 4), 4, filter_planes)
    lift = math.tanh(sharpness * threshold)
    scale = lift + math.tanh(sharpness * (1.0 - threshold))

    def gathered(source, plane):
        return (
            source[0, plane]
            + (source[1, plane - 1] + source[1, plane + 1])
            + (source[2, plane - 2] + source[2, plane + 2])
        )

    def material(chunk):
        for step in chunk:
            at = step - 3
            plane = step + 2
            weight = inside_x(at) * masks[1]
            weight = weight + (inside_x(at - 1) + inside_x(at + 1)) * masks[2]
            weight = weight + (inside_x(at - 2) + inside_x(at + 2)) * masks[3]
            weight = 1.0 / jnp.maximum(weight, 1.0)
            smoothed = gathered(cone, plane)
            smoothed = jnp.concatenate([patched(smoothed, count_t), smoothed[rows:]], 0)
            tanh_shift = jnp.tanh(sharpness * (smoothed * weight - threshold))
            density = (lift + tanh_shift) * (1.0 / scale)
            flag = flags[(at + BRICK) // BRICK]
            squared = density * density
            moduli[step] = (young_floor + (1.0 - young_floor) * (squared * density)) * flag
            slope = (1.0 - tanh_shift * tanh_shift) * weight
            factor[step] = (
                (-3.0 * (1.0 - young_floor) * sharpness / scale) * (squared * flag) * slope
            )

            @pl.when((at >= 0) & (at < size_x))
            def _():
                dens_out[lax.clamp(0, at, size_x - 1)] = density[:size_y]

    chunks = jnp.where(at_side, (size_x + 6) // 4, (size_x + 9) // 4)
    in_chunks(begin, chunks, 4, material)

    first_modes = plane_modes([field[comp + 1, begin + 2] for comp in range(3)], rows)
    for number, key in enumerate(KEYS):
        held[number] = first_modes[key]
        carry[number] = jnp.zeros((full, lanes), f32)

    def operate(chunk):
        old = {key: held[number] for number, key in enumerate(KEYS)}
        above = {key: carry[number] for number, key in enumerate(KEYS)}
        for step in chunk:
            new = plane_modes([field[comp + 1, step + 3] for comp in range(3)], rows)
            modes = element_modes(old, new)
            old = new
            stiff = moduli[step]
            forces = modal_product(modal, modes)
            at_node = {}
            for key in KEYS:
                even, odd = forces[key_row(0, key)], forces[key_row(1, key)]
                odd = odd * stiff
                even = jnp.zeros_like(odd) if even is None else even * stiff
                at_node[key] = above[key] + (even - odd)
                above[key] = even + odd
            mask = masks[0] * inside_x(step - 3)
            for comp in range(3):
                along = []
                for mode_z in range(2):
                    even, odd = at_node[(comp, 0, mode_z)], at_node[(comp, 1, mode_z)]
                    along.append((even - odd) + roll_rows(even + odd, 1, rows))
                total = (along[0] - along[1]) + roll(along[0] + along[1], 1)
                total = (total + spring_rate * field[comp + 1, step + 2]) * mask
                applied[comp, step, :rows] = patched(total, count_t)
                applied[comp, step, rows:] = total[rows:]
        for number, key in enumerate(KEYS):
            held[number] = old[key]
            carry[number] = above[key]

    in_chunks(begin, chunks, 4, operate)

    first_modes = plane_modes([applied[comp, 3] for comp in range(3)], size_y)
    for number, key in enumerate(KEYS):
        small_held[number] = first_modes[key]

    def products(number, sums):
        rr, rs, ss, es = sums
        old = {key: small_held[number] for number, key in enumerate(KEYS)}
        for at in range(4):
            step = number * 4 + at
            for comp in range(3):
                res = field[comp + 1, step + HALO, :size_y]
                app = applied[comp, step + 3, :size_y]
                rr, rs, ss = rr + res * res, rs + res * app, ss + app * app
            new = plane_modes([applied[comp, step + 4] for comp in range(3)], size_y)
            energy = modal_energy(modal, element_modes(old, new))
            old = new
            es = es + energy * shorten(moduli[step + 3], size_y)
        for number, key in enumerate(KEYS):
            small_held[number] = old[key]
        return rr, rs, ss, es

    nothing = jnp.zeros((size_y, size_z), f32)
    most = jnp.zeros((size_y + PAD, size_z), f32)
    sums = list(lax.fori_loop(0, size_x // 4, products, (nothing, nothing, nothing, most)))
    lane_main = lax.broadcasted_iota(jnp.int32, (size_y, lanes), 1)
    strain = jnp.where(lane_main < size_z - 1, sums[3][:size_y], 0.0)
    ends = (in_group == 3 * PAD - 1) & (lane_of < size_y // PAD * group)
    sums[3] = jnp.concatenate([strain, jnp.where(ends, sums[3][size_y:], 0.0)], 0)
    row8 = lax.broadcasted_iota(jnp.int32, (8, LANES), 0)
    tile = jnp.zeros((8, LANES), f32)
    for number, value in enumerate(sums):
        line = jnp.sum(value, axis=0, keepdims=True)
        tile = jnp.where(row8 == number, line, tile)

    def all_sum(slots, partner, count, send, recv):
        copies = [
            pltpu.make_async_remote_copy(
                src_ref=slots.at[0], dst_ref=slots.at[step], send_sem=send.at[step],
                recv_sem=recv.at[step], device_id=partner(step), device_id_type=MESH,
            )
            for step in range(1, count)
        ]
        for copy in copies:
            copy.start()
        total = slots[0]
        for step, copy in enumerate(copies):
            copy.wait_recv()
            total = total + slots[step + 1]
        for copy in copies:
            copy.wait_send()
        return total

    part_z[0] = tile
    part_xy[0] = all_sum(part_z, z_partner, count_z, z_send, z_recv)
    total = all_sum(part_xy, xy_partner, count_x * count_y, xy_send, xy_recv)
    total = jnp.sum(total, axis=1, keepdims=True)
    rr, rs, ss, es = (total[number : number + 1] for number in range(4))
    st = es + spring_rate * ss
    step_first = rr / rs
    rr_next = step_first * step_first * ss - rr
    product = rs - 2.0 * step_first * ss + step_first * step_first * st
    ratio = rr_next / rr
    step_second = rr_next / (product - ratio * rr_next / step_first)
    by_load = step_first + step_second * (1.0 + ratio)
    by_applied = -step_first * step_second

    def displaced(comp, plane):
        return by_load * field[comp + 1, plane + 2] + by_applied * applied[comp, plane]

    for far_x in range(3):
        for side, spot in ((first, 0), (last, size_x + 2)):

            @pl.when(side)
            def _():
                pushed[far_x, spot : spot + 2] = jnp.zeros((2, size_y + PAD, size_z), f32)

    first_modes = plane_modes([displaced(comp, begin + 1) for comp in range(3)], rows)
    for number, key in enumerate(KEYS):
        held[number] = first_modes[key]

    def energies(chunk):
        old = {key: held[number] for number, key in enumerate(KEYS)}
        for step in chunk:
            new = plane_modes([displaced(comp, step + 2) for comp in range(3)], rows)
            push = modal_energy(modal, element_modes(old, new)) * factor[step + 1]
            old = new
            for far_x, value in enumerate(cone_planes(table, push, size_y)):
                pushed[far_x, step] = value
        for number, key in enumerate(KEYS):
            held[number] = old[key]

    in_chunks(begin, jnp.where(at_side, (size_x + 7) // 6, (size_x + 9) // 6), 6, energies)

    def finish(chunk):
        for plane in chunk:
            sens_out[plane] = patched(gathered(pushed, plane + 2), count_t)
            for comp in range(3):
                disp_out[comp, plane] = displaced(comp, plane + 3)[:size_y]

    in_chunks(0, size_x // 4, 4, finish)


def solution(mesh):
    counts = tuple(mesh.shape[name] for name in ("gx", "gy", "gz"))
    placed = (P(None, "gx", "gy", "gz"), P("gx", "gy", "gz"), P())

    def body(load_field, design, solid_map):
        size_x, size_y, size_z = design.shape
        rows = size_y + 2 * PAD
        full, lanes = rows + PAD, size_z
        planes = size_x + 2 * HALO
        f32 = jnp.float32
        vmem = pl.BlockSpec(memory_space=pltpu.VMEM)
        anywhere = pl.BlockSpec(memory_space=pl.ANY)
        pairs = counts[0] * counts[1]
        dma = pltpu.SemaphoreType.DMA

        def run(*refs):
            kernel(counts, *refs)

        return pl.pallas_call(
            run,
            out_shape=(
                jax.ShapeDtypeStruct(load_field.shape, f32),
                jax.ShapeDtypeStruct(design.shape, f32),
                jax.ShapeDtypeStruct(design.shape, f32),
            ),
            in_specs=[anywhere, anywhere, pl.BlockSpec(memory_space=pltpu.SMEM)],
            out_specs=(vmem, vmem, vmem),
            scratch_shapes=[
                pltpu.VMEM((4, planes + 2, full, lanes), f32),
                pltpu.VMEM((3, size_x + 10, full, lanes), f32),
                pltpu.VMEM((size_x + 10, full, lanes), f32),
                pltpu.VMEM((size_x + 10, full, lanes), f32),
                pltpu.VMEM((size_x // BRICK + 2, full, lanes), f32),
                pltpu.VMEM((3, planes + 6, full, lanes), f32),
                pltpu.VMEM((3, size_x + 8, size_y + PAD, size_z), f32),
                pltpu.VMEM((12, full, lanes), f32),
                pltpu.VMEM((12, full, lanes), f32),
                pltpu.VMEM((12, size_y + PAD, size_z), f32),
                pltpu.VMEM((4, planes, PAD, LANES), f32),
                pltpu.VMEM((2, 4, planes, PAD, LANES), f32),
                pltpu.VMEM((4, full, lanes), f32),
                pltpu.VMEM((counts[2], 8, LANES), f32),
                pltpu.VMEM((pairs, 8, LANES), f32),
                dma((6,)),
                dma((6,)),
                dma((counts[2],)),
                dma((counts[2],)),
                dma((pairs,)),
                dma((pairs,)),
                dma((4,)),
            ],
            compiler_params=pltpu.CompilerParams(
                collective_id=0, has_side_effects=True, vmem_limit_bytes=40 * 2**20
            ),
        )(load_field, design, solid_map)

    return jax.shard_map(
        body,
        mesh=mesh,
        in_specs=placed,
        out_specs=(P(None, "gx", "gy", "gz"), P("gx", "gy", "gz"), P("gx", "gy", "gz")),
        check_vma=False,
    )
```

```python
import itertools
import math

import jax
import jax.numpy as jnp
import numpy as np
from jax import lax
from jax.experimental import pallas as pl
from jax.experimental.pallas import tpu as pltpu
from jax.sharding import PartitionSpec as P

BRICK = 16
HALO = 5
PAD = 8
LANES = 128

young_floor = 0.001
spring_rate = 0.05
sharpness = 8.0
threshold = 0.5
poisson = 0.3
MESH = pl.DeviceIdType.MESH


def element_matrix():
    lame_first = poisson / ((1.0 + poisson) * (1.0 - 2.0 * poisson))
    shear_mod = 1.0 / (2.0 * (1.0 + poisson))
    elastic = np.zeros((6, 6))
    elastic[:3, :3] = lame_first
    for axis_one in range(3):
        elastic[axis_one, axis_one] += 2.0 * shear_mod
        elastic[axis_one + 3, axis_one + 3] = shear_mod
    gauss_point = 1.0 / math.sqrt(3.0)
    stiffness = np.zeros((24, 24))
    for point_x in (-gauss_point, gauss_point):
        for point_y in (-gauss_point, gauss_point):
            for point_z in (-gauss_point, gauss_point):
                strain = np.zeros((6, 24))
                for corner in range(8):
                    sign_a = 2 * (corner // 4) - 1
                    sign_b = 2 * (corner // 2 % 2) - 1
                    sign_c = 2 * (corner % 2) - 1
                    along_x = 0.25 * sign_a * (1 + sign_b * point_y) * (1 + sign_c * point_z)
                    along_y = 0.25 * (1 + sign_a * point_x) * sign_b * (1 + sign_c * point_z)
                    along_z = 0.25 * (1 + sign_a * point_x) * (1 + sign_b * point_y) * sign_c
                    column = 3 * corner
                    strain[0, column] = along_x
                    strain[1, column + 1] = along_y
                    strain[2, column + 2] = along_z
                    strain[3, column + 1] = along_z
                    strain[3, column + 2] = along_y
                    strain[4, column] = along_z
                    strain[4, column + 2] = along_x
                    strain[5, column] = along_y
                    strain[5, column + 1] = along_x
                stiffness += strain.T @ elastic @ strain * 0.125
    return stiffness


def cone_offsets():
    listed = []
    for step_x in range(-2, 3):
        for step_y in range(-2, 3):
            for step_z in range(-2, 3):
                radius = step_x * step_x + step_y * step_y + step_z * step_z
                if radius < 9:
                    listed.append((step_x, step_y, step_z, 3.0 - math.sqrt(radius)))
    return listed


def modal_matrix():
    stiffness = element_matrix()
    change = np.zeros((24, 24))
    for mode in itertools.product((0, 1), repeat=3):
        for corner in itertools.product((0, 1), repeat=3):
            sign = 1.0
            for is_diff, side in zip(mode, corner):
                sign *= (2 * side - 1) if is_diff else 1
            for comp in range(3):
                row = 3 * (4 * mode[0] + 2 * mode[1] + mode[2]) + comp
                change[row, 3 * (4 * corner[0] + 2 * corner[1] + corner[2]) + comp] = sign
    modal = change @ stiffness @ change.T / 64.0
    modal[np.abs(modal) < 1e-10] = 0.0
    return modal


def cone_table():
    table = {}
    for step_x, step_y, step_z, weight in cone_offsets():
        if min(step_x, step_y, step_z) >= 0:
            table[(step_x, step_y, step_z)] = weight
    return table


MODES = tuple(itertools.product((0, 1), repeat=2))


def roll(value, shift):
    return pltpu.roll(value, shift % value.shape[1], 1)


def tiles_of(value):
    return [value[at : at + PAD] for at in range(0, value.shape[0], PAD)]


def shift_tile(tiles, at, shift):
    count = len(tiles) - 1
    if at == count:
        group = LANES // count
        other = roll(tiles[at], group if shift > 0 else -group)
    else:
        other = tiles[(at - 1) % count] if shift > 0 else tiles[(at + 1) % count]
    row = lax.broadcasted_iota(jnp.int32, (PAD, LANES), 0)
    far = row >= PAD - shift if shift > 0 else row < -shift
    return pltpu.roll(jnp.where(far, other, tiles[at]), shift % PAD, 0)


def z_parts(values):
    out = {}
    for comp, value in enumerate(values):
        tiles = tiles_of(value)
        ahead = [roll(tile, -1) for tile in tiles]
        out[(comp, 0)] = [tile + other for tile, other in zip(tiles, ahead)]
        out[(comp, 1)] = [other - tile for tile, other in zip(tiles, ahead)]
    return out


def tile_modes(parts, at):
    out = {}
    for (comp, mode_z), tiles in parts.items():
        above = shift_tile(tiles, at, -1)
        out[(comp, 0, mode_z)] = tiles[at] + above
        out[(comp, 1, mode_z)] = above - tiles[at]
    return out


def patched(value, count):
    edge = value[-PAD:]
    height = value.shape[0] - PAD
    group = LANES // count
    lane = lax.broadcasted_iota(jnp.int32, edge.shape, 1)
    out = []
    for tile in range(height // PAD):
        low = roll(edge, -(tile * group + PAD))
        high = roll(edge, LANES - 3 * PAD - tile * group)
        mine = jnp.where(lane < 2, low, value[tile * PAD : (tile + 1) * PAD])
        out.append(jnp.where(lane >= LANES - 3, high, mine))
    return jnp.concatenate(out, 0)


def modal_product(modal, modes):
    out = {}
    for row in range(24):
        total = None
        for col in range(24):
            if modal[row, col] != 0.0:
                term = modes[col] * float(modal[row, col])
                total = term if total is None else total + term
        out[row] = total
    return out


def key_row(mode_x, key):
    comp, mode_y, mode_z = key
    return 3 * (4 * mode_x + 2 * mode_y + mode_z) + comp


KEYS = tuple((comp, my, mz) for comp in range(3) for my, mz in MODES)


def element_modes(old, new):
    modes = {}
    for key in KEYS:
        modes[key_row(0, key)] = old[key] + new[key]
        modes[key_row(1, key)] = new[key] - old[key]
    return modes


def modal_energy(modal, modes):
    forces = modal_product(modal, modes)
    total = None
    for row in range(24):
        if forces[row] is not None:
            term = forces[row] * modes[row]
            total = term if total is None else total + term
    return total


def cone_tiles(table, tiles, chosen):
    along_z = (
        tiles,
        [roll(tile, 1) + roll(tile, -1) for tile in tiles],
        [roll(tile, 2) + roll(tile, -2) for tile in tiles],
    )
    out = []
    for at in chosen:
        sums = [None, None, None]
        for far_z, part in enumerate(along_z):
            along_y = (
                part[at],
                shift_tile(part, at, 1) + shift_tile(part, at, -1),
                shift_tile(part, at, 2) + shift_tile(part, at, -2),
            )
            for far_x in range(3):
                for far_y in range(3):
                    weight = table.get((far_x, far_y, far_z))
                    if weight is not None:
                        term = along_y[far_y] * weight
                        sums[far_x] = term if sums[far_x] is None else sums[far_x] + term
        out.append(sums)
    return out


def in_chunks(begin, chunks, size, body):
    def step(number, _):
        body([begin + number * size + at for at in range(size)])
        return 0

    lax.fori_loop(0, chunks, step, 0)


def kernel(
    counts,
    load,
    design,
    solid,
    disp_out,
    sens_out,
    dens_out,
    field,
    applied,
    moduli,
    factor,
    flags,
    cone,
    pushed,
    held,
    carry,
    packed,
    arrived,
    masks,
    part_z,
    part_xy,
    face_send,
    face_recv,
    z_send,
    z_recv,
    xy_send,
    xy_recv,
    copy_sem,
):
    count_x, count_y, count_z = counts
    size_x, size_y, size_z = design.shape
    rows = size_y + 2 * PAD
    full, lanes = rows + PAD, size_z
    count_t = rows // PAD
    group = LANES // count_t
    planes = size_x + 2 * HALO
    first, last = lax.axis_index("gx") == 0, lax.axis_index("gx") == count_x - 1
    ix, iy, iz = lax.axis_index("gx"), lax.axis_index("gy"), lax.axis_index("gz")
    modal = modal_matrix()
    table = cone_table()
    f32 = jnp.float32

    def z_partner(step):
        return (ix, iy, lax.rem(iz + step, count_z))

    def xy_partner(step):
        spot = lax.rem(ix * count_y + iy + step, count_x * count_y)
        return (spot // count_y, lax.rem(spot, count_y), iz)

    inner = pl.ds(HALO, size_x)
    bring = [pltpu.make_async_copy(design, field.at[0, inner, pl.ds(0, size_y)], copy_sem.at[0])]
    for comp in range(3):
        bring.append(
            pltpu.make_async_copy(
                load.at[comp], field.at[comp + 1, inner, pl.ds(0, size_y)], copy_sem.at[comp + 1]
            )
        )
    for copy in bring:
        copy.start()

    for index in range(4):

        def clear(plane, _):
            field[index, plane + HALO, size_y:rows] = jnp.zeros((rows - size_y, lanes), f32)
            return 0

        lax.fori_loop(0, size_x, clear, 0)
        for plane in range(HALO):
            field[index, plane, :rows] = jnp.zeros((rows, lanes), f32)
            field[index, plane + HALO + size_x, :rows] = jnp.zeros((rows, lanes), f32)

    @pl.when(iz == 0)
    def _():
        arrived[1] = jnp.zeros(arrived.shape[1:], f32)

    @pl.when(iz == count_z - 1)
    def _():
        arrived[0] = jnp.zeros(arrived.shape[1:], f32)

    barrier = pltpu.get_barrier_semaphore()
    for step in range(1, count_z):
        pl.semaphore_signal(barrier, inc=1, device_id=z_partner(step), device_id_type=MESH)
    for step in range(1, count_x * count_y):
        pl.semaphore_signal(barrier, inc=1, device_id=xy_partner(step), device_id_type=MESH)
    pl.semaphore_wait(barrier, count_z - 1 + count_x * count_y - 1)
    for copy in bring:
        copy.wait()

    def exchange(slot, down, up, down_id, up_id, has_down, has_up):
        to_down = pltpu.make_async_remote_copy(
            src_ref=down[0], dst_ref=down[1], send_sem=face_send.at[slot],
            recv_sem=face_recv.at[slot], device_id=down_id, device_id_type=MESH,
        )
        to_up = pltpu.make_async_remote_copy(
            src_ref=up[0], dst_ref=up[1], send_sem=face_send.at[slot + 1],
            recv_sem=face_recv.at[slot + 1], device_id=up_id, device_id_type=MESH,
        )

        @pl.when(has_down)
        def _():
            to_down.start()

        @pl.when(has_up)
        def _():
            to_up.start()

        @pl.when(has_up)
        def _():
            to_down.wait_recv()
            to_up.wait_send()

        @pl.when(has_down)
        def _():
            to_up.wait_recv()
            to_down.wait_send()

    main = pl.ds(0, size_z)
    exchange(
        0,
        (field.at[:, inner, pl.ds(0, PAD), main], field.at[:, inner, pl.ds(size_y, PAD), main]),
        (
            field.at[:, inner, pl.ds(size_y - PAD, PAD), main],
            field.at[:, inner, pl.ds(size_y + PAD, PAD), main],
        ),
        (ix, lax.max(iy - 1, 0), iz),
        (ix, lax.min(iy + 1, count_y - 1), iz),
        iy > 0,
        iy < count_y - 1,
    )
    every = pl.ds(0, rows)
    exchange(
        2,
        (
            field.at[:, pl.ds(HALO, HALO), every, main],
            field.at[:, pl.ds(HALO + size_x, HALO), every, main],
        ),
        (field.at[:, pl.ds(size_x, HALO), every, main], field.at[:, pl.ds(0, HALO), every, main]),
        (lax.max(ix - 1, 0), iy, iz),
        (lax.min(ix + 1, count_x - 1), iy, iz),
        ix > 0,
        ix < count_x - 1,
    )

    lane_of = lax.broadcasted_iota(jnp.int32, (PAD, LANES), 1)
    in_group = lax.rem(lane_of, group)

    def pack(chunk):
        for plane, index in itertools.product(chunk, range(4)):
            out = jnp.zeros((PAD, LANES), f32)
            for tile in range(count_t):
                at = tile * group
                mine = field[index, plane, tile * PAD : (tile + 1) * PAD]
                here = (lane_of >= at + PAD) & (lane_of < at + 2 * PAD)
                out = jnp.where(here, roll(mine, at + PAD), out)
                here = (lane_of >= at + 2 * PAD) & (lane_of < at + 3 * PAD)
                out = jnp.where(here, roll(mine, at + 3 * PAD), out)
            packed[index, plane] = out

    in_chunks(0, planes // 2, 2, pack)
    exchange(
        4,
        (packed, arrived.at[0]),
        (packed, arrived.at[1]),
        (ix, iy, lax.max(iz - 1, 0)),
        (ix, iy, lax.min(iz + 1, count_z - 1)),
        iz > 0,
        iz < count_z - 1,
    )

    def unpack(chunk):
        for plane, index in itertools.product(chunk, range(4)):
            below = roll(arrived[1, index, plane], -2 * PAD)
            above = roll(arrived[0, index, plane], 2 * PAD)
            value = jnp.where(in_group < PAD, below, packed[index, plane])
            field[index, plane, rows:] = jnp.where(in_group >= 3 * PAD, above, value)

    in_chunks(0, planes // 2, 2, unpack)

    row_at = lax.broadcasted_iota(jnp.int32, (rows, lanes), 0)
    lane_at = lax.broadcasted_iota(jnp.int32, (rows, lanes), 1)
    edge_row = lax.broadcasted_iota(jnp.int32, (PAD, lanes), 0) + lane_of // group * PAD
    edge_lane = jnp.where(in_group < 2 * PAD, in_group - PAD, in_group + size_z - 3 * PAD)
    row_at = jnp.concatenate([row_at, edge_row], 0)
    lane_at = jnp.concatenate([lane_at, edge_lane], 0) + iz * size_z
    row_at = jnp.where(row_at < size_y + PAD, row_at, row_at - rows) + iy * size_y
    inside_yz = (
        (row_at >= 0) & (row_at < size_y * count_y) & (lane_at >= 0) & (lane_at < size_z * count_z)
    )
    masks[0] = jnp.where(inside_yz, 1.0, 0.0).astype(f32)
    for far_x, tiles in enumerate(zip(*cone_tiles(table, tiles_of(masks[0]), range(count_t + 1)))):
        value = jnp.concatenate(tiles, 0)
        masks[1 + far_x, :rows] = patched(value, count_t)
        masks[1 + far_x, rows:] = value[rows:]

    def inside_x(plane):
        where = plane + ix * size_x
        return jnp.where((where >= 0) & (where < size_x * count_x), 1.0, 0.0).astype(f32)

    bricks_x, bricks_y, bricks_z = size_x // BRICK, size_y // BRICK, size_z // BRICK

    def brick(bx, by, bz):
        gx, gy, gz = ix * bricks_x + bx, iy * bricks_y + by, iz * bricks_z + bz
        top_x, top_y, top_z = bricks_x * count_x, bricks_y * count_y, bricks_z * count_z
        good = (gx >= 0) & (gx < top_x) & (gy >= 0) & (gy < top_y) & (gz >= 0) & (gz < top_z)
        value = solid[
            lax.clamp(0, gx, top_x - 1), lax.clamp(0, gy, top_y - 1), lax.clamp(0, gz, top_z - 1)
        ]
        return value.astype(f32) * jnp.where(good, 1.0, 0.0).astype(f32)

    for bx in range(-1, bricks_x + 1):
        edge = jnp.zeros((PAD, lanes), f32)
        for by in range(-1, bricks_y + 1):
            line = jnp.zeros((PAD, lanes), f32)
            for bz in range(bricks_z):
                here = (lane_of >= bz * BRICK) & (lane_of < (bz + 1) * BRICK)
                line = jnp.where(here, brick(bx, by, bz), line)
            if by < 0:
                spots = [size_y + PAD]
            elif by == bricks_y:
                spots = [size_y]
            else:
                spots = range(by * BRICK, (by + 1) * BRICK, PAD)
            around = jnp.zeros((PAD, lanes), f32)
            for part, bz in enumerate((-1, 0, bricks_z - 1, bricks_z)):
                around = jnp.where(in_group >= part * PAD, brick(bx, by, bz), around)
            for spot in spots:
                flags[bx + 1, spot : spot + PAD, :] = line
                edge = jnp.where(lane_of // group == spot // PAD, around, edge)
        flags[bx + 1, rows:, :] = edge

    begin = jnp.where(first, 2, 0)
    at_side = first | last

    all_tiles = range(count_t + 1)
    own_tiles = (*range(size_y // PAD), count_t)

    def filter_planes(chunk):
        for plane in chunk:
            for at, sums in enumerate(cone_tiles(table, tiles_of(field[0, plane]), all_tiles)):
                for far_x in range(3):
                    cone[far_x, plane, at * PAD : (at + 1) * PAD] = sums[far_x]

    in_chunks(begin, jnp.where(at_side, (planes + 1) // 4, (planes + 3) // 4), 4, filter_planes)
    lift = math.tanh(sharpness * threshold)
    scale = lift + math.tanh(sharpness * (1.0 - threshold))

    def gathered(source, plane):
        return (
            source[0, plane]
            + (source[1, plane - 1] + source[1, plane + 1])
            + (source[2, plane - 2] + source[2, plane + 2])
        )

    def material(chunk):
        for step in chunk:
            at = step - 3
            plane = step + 2
            weight = inside_x(at) * masks[1]
            weight = weight + (inside_x(at - 1) + inside_x(at + 1)) * masks[2]
            weight = weight + (inside_x(at - 2) + inside_x(at + 2)) * masks[3]
            weight = 1.0 / jnp.maximum(weight, 1.0)
            smoothed = gathered(cone, plane)
            smoothed = jnp.concatenate([patched(smoothed, count_t), smoothed[rows:]], 0)
            tanh_shift = jnp.tanh(sharpness * (smoothed * weight - threshold))
            density = (lift + tanh_shift) * (1.0 / scale)
            flag = flags[(at + BRICK) // BRICK]
            squared = density * density
            moduli[step] = (young_floor + (1.0 - young_floor) * (squared * density)) * flag
            slope = (1.0 - tanh_shift * tanh_shift) * weight
            factor[step] = (
                (-3.0 * (1.0 - young_floor) * sharpness / scale) * (squared * flag) * slope
            )

            @pl.when((at >= 0) & (at < size_x))
            def _():
                dens_out[lax.clamp(0, at, size_x - 1)] = density[:size_y]

    chunks = jnp.where(at_side, (size_x + 6) // 4, (size_x + 9) // 4)
    in_chunks(begin, chunks, 4, material)

    def start(values, chosen):
        parts = z_parts(values)
        for at in chosen:
            modes = tile_modes(parts, at)
            for number, key in enumerate(KEYS):
                held[number, at * PAD : (at + 1) * PAD] = modes[key]

    start([field[comp + 1, begin + 2] for comp in range(3)], all_tiles)
    carry[...] = jnp.zeros_like(carry)

    def operate(chunk):
        parts = [z_parts([field[comp + 1, step + 3] for comp in range(3)]) for step in chunk]
        moved = [{} for _ in chunk]
        stays = [{} for _ in chunk]
        for at in all_tiles:
            spot = slice(at * PAD, (at + 1) * PAD)
            old = {key: held[number, spot] for number, key in enumerate(KEYS)}
            above = {key: carry[number, spot] for number, key in enumerate(KEYS)}
            for place, step in enumerate(chunk):
                new = tile_modes(parts[place], at)
                forces = modal_product(modal, element_modes(old, new))
                old = new
                stiff = moduli[step, spot]
                at_node = {}
                for key in KEYS:
                    even, odd = forces[key_row(0, key)], forces[key_row(1, key)]
                    odd = odd * stiff
                    if even is None:
                        at_node[key] = above[key] - odd
                        above[key] = odd
                    else:
                        even = even * stiff
                        at_node[key] = above[key] + (even - odd)
                        above[key] = even + odd
                for comp, mode_z in itertools.product(range(3), range(2)):
                    even, odd = at_node[(comp, 0, mode_z)], at_node[(comp, 1, mode_z)]
                    moved[place].setdefault((comp, mode_z), []).append(even + odd)
                    stays[place].setdefault((comp, mode_z), []).append(even - odd)
            for number, key in enumerate(KEYS):
                held[number, spot] = old[key]
                carry[number, spot] = above[key]
        for place, step in enumerate(chunk):
            known = inside_x(step - 3)
            for comp in range(3):
                totals = []
                for at in all_tiles:
                    spot = slice(at * PAD, (at + 1) * PAD)
                    along = [
                        stays[place][(comp, mode_z)][at]
                        + shift_tile(moved[place][(comp, mode_z)], at, 1)
                        for mode_z in range(2)
                    ]
                    total = (along[0] - along[1]) + roll(along[0] + along[1], 1)
                    total = total + spring_rate * field[comp + 1, step + 2, spot]
                    totals.append(total * (masks[0, spot] * known))
                total = jnp.concatenate(totals, 0)
                applied[comp, step, :rows] = patched(total, count_t)
                applied[comp, step, rows:] = totals[-1]

    in_chunks(begin, chunks, 4, operate)

    start([applied[comp, 3] for comp in range(3)], own_tiles)

    def products(number, sums):
        rr, rs, ss, es = sums
        chunk = [number * 4 + at for at in range(4)]
        parts = [z_parts([applied[comp, step + 4] for comp in range(3)]) for step in chunk]
        for step, comp in itertools.product(chunk, range(3)):
            res = field[comp + 1, step + HALO, :size_y]
            app = applied[comp, step + 3, :size_y]
            rr, rs, ss = rr + res * res, rs + res * app, ss + app * app
        strain = tiles_of(es)
        for number, at in enumerate(own_tiles):
            spot = slice(at * PAD, (at + 1) * PAD)
            old = {key: held[number, spot] for number, key in enumerate(KEYS)}
            for place, step in enumerate(chunk):
                new = tile_modes(parts[place], at)
                energy = modal_energy(modal, element_modes(old, new))
                old = new
                strain[number] = strain[number] + energy * moduli[step + 3, spot]
            for key_number, key in enumerate(KEYS):
                held[key_number, spot] = old[key]
        return rr, rs, ss, jnp.concatenate(strain, 0)

    nothing = jnp.zeros((size_y, size_z), f32)
    most = jnp.zeros((size_y + PAD, size_z), f32)
    sums = list(lax.fori_loop(0, size_x // 4, products, (nothing, nothing, nothing, most)))
    lane_main = lax.broadcasted_iota(jnp.int32, (size_y, lanes), 1)
    strain = jnp.where(lane_main < size_z - 1, sums[3][:size_y], 0.0)
    ends = (in_group == 3 * PAD - 1) & (lane_of < size_y // PAD * group)
    sums[3] = jnp.concatenate([strain, jnp.where(ends, sums[3][size_y:], 0.0)], 0)
    row8 = lax.broadcasted_iota(jnp.int32, (8, LANES), 0)
    tile = jnp.zeros((8, LANES), f32)
    for number, value in enumerate(sums):
        line = jnp.sum(value, axis=0, keepdims=True)
        tile = jnp.where(row8 == number, line, tile)

    def all_sum(slots, partner, count, send, recv):
        copies = [
            pltpu.make_async_remote_copy(
                src_ref=slots.at[0], dst_ref=slots.at[step], send_sem=send.at[step],
                recv_sem=recv.at[step], device_id=partner(step), device_id_type=MESH,
            )
            for step in range(1, count)
        ]
        for copy in copies:
            copy.start()
        total = slots[0]
        for step, copy in enumerate(copies):
            copy.wait_recv()
            total = total + slots[step + 1]
        for copy in copies:
            copy.wait_send()
        return total

    part_z[0] = tile
    part_xy[0] = all_sum(part_z, z_partner, count_z, z_send, z_recv)
    total = all_sum(part_xy, xy_partner, count_x * count_y, xy_send, xy_recv)
    total = jnp.sum(total, axis=1, keepdims=True)
    rr, rs, ss, es = (total[number : number + 1] for number in range(4))
    st = es + spring_rate * ss
    step_first = rr / rs
    rr_next = step_first * step_first * ss - rr
    product = rs - 2.0 * step_first * ss + step_first * step_first * st
    ratio = rr_next / rr
    step_second = rr_next / (product - ratio * rr_next / step_first)
    by_load = step_first + step_second * (1.0 + ratio)
    by_applied = -step_first * step_second

    def displaced(comp, plane):
        return by_load * field[comp + 1, plane + 2] + by_applied * applied[comp, plane]

    for far_x in range(3):
        for side, spot in ((first, 0), (last, size_x + 2)):

            @pl.when(side)
            def _():
                pushed[far_x, spot : spot + 2] = jnp.zeros((2, size_y + PAD, size_z), f32)

    start([displaced(comp, begin + 1) for comp in range(3)], all_tiles)

    def energies(chunk):
        parts = [z_parts([displaced(comp, step + 2) for comp in range(3)]) for step in chunk]
        pushes = [[] for _ in chunk]
        for at in all_tiles:
            spot = slice(at * PAD, (at + 1) * PAD)
            old = {key: held[number, spot] for number, key in enumerate(KEYS)}
            for place, step in enumerate(chunk):
                new = tile_modes(parts[place], at)
                energy = modal_energy(modal, element_modes(old, new))
                old = new
                pushes[place].append(energy * factor[step + 1, spot])
            for number, key in enumerate(KEYS):
                held[number, spot] = old[key]
        for place, step in enumerate(chunk):
            for number, sums in enumerate(cone_tiles(table, pushes[place], own_tiles)):
                for far_x in range(3):
                    pushed[far_x, step, number * PAD : (number + 1) * PAD] = sums[far_x]

    in_chunks(begin, jnp.where(at_side, (size_x + 7) // 6, (size_x + 9) // 6), 6, energies)

    def finish(chunk):
        for plane in chunk:
            sens_out[plane] = patched(gathered(pushed, plane + 2), count_t)
            for comp in range(3):
                disp_out[comp, plane] = displaced(comp, plane + 3)[:size_y]

    in_chunks(0, size_x // 4, 4, finish)


def solution(mesh):
    counts = tuple(mesh.shape[name] for name in ("gx", "gy", "gz"))
    placed = (P(None, "gx", "gy", "gz"), P("gx", "gy", "gz"), P())

    def body(load_field, design, solid_map):
        size_x, size_y, size_z = design.shape
        rows = size_y + 2 * PAD
        full, lanes = rows + PAD, size_z
        planes = size_x + 2 * HALO
        f32 = jnp.float32
        vmem = pl.BlockSpec(memory_space=pltpu.VMEM)
        anywhere = pl.BlockSpec(memory_space=pltpu.HBM)
        pairs = counts[0] * counts[1]
        dma = pltpu.SemaphoreType.DMA

        def run(*refs):
            kernel(counts, *refs)

        return pl.pallas_call(
            run,
            out_shape=(
                jax.ShapeDtypeStruct(load_field.shape, f32),
                jax.ShapeDtypeStruct(design.shape, f32),
                jax.ShapeDtypeStruct(design.shape, f32),
            ),
            in_specs=[anywhere, anywhere, pl.BlockSpec(memory_space=pltpu.SMEM)],
            out_specs=(vmem, vmem, vmem),
            scratch_shapes=[
                pltpu.VMEM((4, planes + 2, full, lanes), f32),
                pltpu.VMEM((3, size_x + 10, full, lanes), f32),
                pltpu.VMEM((size_x + 10, full, lanes), f32),
                pltpu.VMEM((size_x + 10, full, lanes), f32),
                pltpu.VMEM((size_x // BRICK + 2, full, lanes), f32),
                pltpu.VMEM((3, planes + 6, full, lanes), f32),
                pltpu.VMEM((3, size_x + 8, size_y + PAD, size_z), f32),
                pltpu.VMEM((12, full, lanes), f32),
                pltpu.VMEM((12, full, lanes), f32),
                pltpu.VMEM((4, planes, PAD, LANES), f32),
                pltpu.VMEM((2, 4, planes, PAD, LANES), f32),
                pltpu.VMEM((4, full, lanes), f32),
                pltpu.VMEM((counts[2], 8, LANES), f32),
                pltpu.VMEM((pairs, 8, LANES), f32),
                dma((6,)),
                dma((6,)),
                dma((counts[2],)),
                dma((counts[2],)),
                dma((pairs,)),
                dma((pairs,)),
                dma((4,)),
            ],
            compiler_params=pltpu.CompilerParams(
                collective_id=0, has_side_effects=True, vmem_limit_bytes=40 * 2**20
            ),
        )(load_field, design, solid_map)

    return jax.shard_map(
        body,
        mesh=mesh,
        in_specs=placed,
        out_specs=(P(None, "gx", "gy", "gz"), P("gx", "gy", "gz"), P("gx", "gy", "gz")),
        check_vma=False,
    )
```

```python
import itertools
import math

import jax
import jax.numpy as jnp
import numpy as np
from jax import lax
from jax.experimental import pallas as pl
from jax.experimental.pallas import tpu as pltpu
from jax.sharding import PartitionSpec as P

BRICK = 16
HALO = 5
PAD = 8
LANES = 128

young_floor = 0.001
spring_rate = 0.05
sharpness = 8.0
threshold = 0.5
poisson = 0.3
MESH = pl.DeviceIdType.MESH


def element_matrix():
    lame_first = poisson / ((1.0 + poisson) * (1.0 - 2.0 * poisson))
    shear_mod = 1.0 / (2.0 * (1.0 + poisson))
    elastic = np.zeros((6, 6))
    elastic[:3, :3] = lame_first
    for axis_one in range(3):
        elastic[axis_one, axis_one] += 2.0 * shear_mod
        elastic[axis_one + 3, axis_one + 3] = shear_mod
    gauss_point = 1.0 / math.sqrt(3.0)
    stiffness = np.zeros((24, 24))
    for point_x in (-gauss_point, gauss_point):
        for point_y in (-gauss_point, gauss_point):
            for point_z in (-gauss_point, gauss_point):
                strain = np.zeros((6, 24))
                for corner in range(8):
                    sign_a = 2 * (corner // 4) - 1
                    sign_b = 2 * (corner // 2 % 2) - 1
                    sign_c = 2 * (corner % 2) - 1
                    along_x = 0.25 * sign_a * (1 + sign_b * point_y) * (1 + sign_c * point_z)
                    along_y = 0.25 * (1 + sign_a * point_x) * sign_b * (1 + sign_c * point_z)
                    along_z = 0.25 * (1 + sign_a * point_x) * (1 + sign_b * point_y) * sign_c
                    column = 3 * corner
                    strain[0, column] = along_x
                    strain[1, column + 1] = along_y
                    strain[2, column + 2] = along_z
                    strain[3, column + 1] = along_z
                    strain[3, column + 2] = along_y
                    strain[4, column] = along_z
                    strain[4, column + 2] = along_x
                    strain[5, column] = along_y
                    strain[5, column + 1] = along_x
                stiffness += strain.T @ elastic @ strain * 0.125
    return stiffness


def cone_offsets():
    listed = []
    for step_x in range(-2, 3):
        for step_y in range(-2, 3):
            for step_z in range(-2, 3):
                radius = step_x * step_x + step_y * step_y + step_z * step_z
                if radius < 9:
                    listed.append((step_x, step_y, step_z, 3.0 - math.sqrt(radius)))
    return listed


def modal_matrix():
    stiffness = element_matrix()
    change = np.zeros((24, 24))
    for mode in itertools.product((0, 1), repeat=3):
        for corner in itertools.product((0, 1), repeat=3):
            sign = 1.0
            for is_diff, side in zip(mode, corner):
                sign *= (2 * side - 1) if is_diff else 1
            for comp in range(3):
                row = 3 * (4 * mode[0] + 2 * mode[1] + mode[2]) + comp
                change[row, 3 * (4 * corner[0] + 2 * corner[1] + corner[2]) + comp] = sign
    modal = change @ stiffness @ change.T / 64.0
    modal[np.abs(modal) < 1e-10] = 0.0
    return modal


def cone_table():
    table = {}
    for step_x, step_y, step_z, weight in cone_offsets():
        if min(step_x, step_y, step_z) >= 0:
            table[(step_x, step_y, step_z)] = weight
    return table


MODES = tuple(itertools.product((0, 1), repeat=2))


def roll(value, shift):
    return pltpu.roll(value, shift % value.shape[1], 1)


def tiles_of(value):
    return [value[at : at + PAD] for at in range(0, value.shape[0], PAD)]


def shift_tile(tiles, at, shift):
    count = len(tiles) - 1
    if at == count:
        group = LANES // count
        other = roll(tiles[at], group if shift > 0 else -group)
    else:
        other = tiles[(at - 1) % count] if shift > 0 else tiles[(at + 1) % count]
    row = lax.broadcasted_iota(jnp.int32, (PAD, LANES), 0)
    far = row >= PAD - shift if shift > 0 else row < -shift
    return pltpu.roll(jnp.where(far, other, tiles[at]), shift % PAD, 0)


def z_parts(values):
    out = {}
    for comp, value in enumerate(values):
        tiles = tiles_of(value)
        ahead = [roll(tile, -1) for tile in tiles]
        out[(comp, 0)] = [tile + other for tile, other in zip(tiles, ahead)]
        out[(comp, 1)] = [other - tile for tile, other in zip(tiles, ahead)]
    return out


def tile_modes(parts, at):
    out = {}
    for (comp, mode_z), tiles in parts.items():
        above = shift_tile(tiles, at, -1)
        out[(comp, 0, mode_z)] = tiles[at] + above
        out[(comp, 1, mode_z)] = above - tiles[at]
    return out


def patched(value, count):
    edge = value[-PAD:]
    height = value.shape[0] - PAD
    group = LANES // count
    lane = lax.broadcasted_iota(jnp.int32, edge.shape, 1)
    out = []
    for tile in range(height // PAD):
        low = roll(edge, -(tile * group + PAD))
        high = roll(edge, LANES - 3 * PAD - tile * group)
        mine = jnp.where(lane < 2, low, value[tile * PAD : (tile + 1) * PAD])
        out.append(jnp.where(lane >= LANES - 3, high, mine))
    return jnp.concatenate(out, 0)


def modal_product(modal, modes):
    out = {}
    for row in range(24):
        total = None
        for col in range(24):
            if modal[row, col] != 0.0:
                term = modes[col] * float(modal[row, col])
                total = term if total is None else total + term
        out[row] = total
    return out


def key_row(mode_x, key):
    comp, mode_y, mode_z = key
    return 3 * (4 * mode_x + 2 * mode_y + mode_z) + comp


KEYS = tuple((comp, my, mz) for comp in range(3) for my, mz in MODES)


def element_modes(old, new):
    modes = {}
    for key in KEYS:
        modes[key_row(0, key)] = old[key] + new[key]
        modes[key_row(1, key)] = new[key] - old[key]
    return modes


def modal_energy(modal, modes):
    forces = modal_product(modal, modes)
    total = None
    for row in range(24):
        if forces[row] is not None:
            term = forces[row] * modes[row]
            total = term if total is None else total + term
    return total


def cone_tiles(table, tiles, chosen):
    along_z = (
        tiles,
        [roll(tile, 1) + roll(tile, -1) for tile in tiles],
        [roll(tile, 2) + roll(tile, -2) for tile in tiles],
    )
    out = []
    for at in chosen:
        sums = [None, None, None]
        for far_z, part in enumerate(along_z):
            along_y = (
                part[at],
                shift_tile(part, at, 1) + shift_tile(part, at, -1),
                shift_tile(part, at, 2) + shift_tile(part, at, -2),
            )
            for far_x in range(3):
                for far_y in range(3):
                    weight = table.get((far_x, far_y, far_z))
                    if weight is not None:
                        term = along_y[far_y] * weight
                        sums[far_x] = term if sums[far_x] is None else sums[far_x] + term
        out.append(sums)
    return out


def in_chunks(begin, chunks, size, body):
    def step(number, _):
        body([begin + number * size + at for at in range(size)])
        return 0

    lax.fori_loop(0, chunks, step, 0)


def kernel(
    counts,
    load,
    design,
    solid,
    disp_out,
    sens_out,
    dens_out,
    field,
    applied,
    moduli,
    factor,
    flags,
    cone,
    pushed,
    held,
    carry,
    packed,
    arrived,
    masks,
    part_z,
    part_xy,
    face_send,
    face_recv,
    z_send,
    z_recv,
    xy_send,
    xy_recv,
    copy_sem,
):
    count_x, count_y, count_z = counts
    size_x, size_y, size_z = design.shape
    rows = size_y + 2 * PAD
    full, lanes = rows + PAD, size_z
    count_t = rows // PAD
    group = LANES // count_t
    planes = size_x + 2 * HALO
    first, last = lax.axis_index("gx") == 0, lax.axis_index("gx") == count_x - 1
    ix, iy, iz = lax.axis_index("gx"), lax.axis_index("gy"), lax.axis_index("gz")
    modal = modal_matrix()
    table = cone_table()
    f32 = jnp.float32

    def z_partner(step):
        return (ix, iy, lax.rem(iz + step, count_z))

    def xy_partner(step):
        spot = lax.rem(ix * count_y + iy + step, count_x * count_y)
        return (spot // count_y, lax.rem(spot, count_y), iz)

    inner = pl.ds(HALO, size_x)
    bring = [pltpu.make_async_copy(design, field.at[0, inner, pl.ds(0, size_y)], copy_sem.at[0])]
    for comp in range(3):
        bring.append(
            pltpu.make_async_copy(
                load.at[comp], field.at[comp + 1, inner, pl.ds(0, size_y)], copy_sem.at[comp + 1]
            )
        )
    for copy in bring:
        copy.start()

    for index in range(4):

        def clear(plane, _):
            field[index, plane + HALO, size_y:rows] = jnp.zeros((rows - size_y, lanes), f32)
            return 0

        lax.fori_loop(0, size_x, clear, 0)
        for plane in range(HALO):
            field[index, plane, :rows] = jnp.zeros((rows, lanes), f32)
            field[index, plane + HALO + size_x, :rows] = jnp.zeros((rows, lanes), f32)

    @pl.when(iz == 0)
    def _():
        arrived[1] = jnp.zeros(arrived.shape[1:], f32)

    @pl.when(iz == count_z - 1)
    def _():
        arrived[0] = jnp.zeros(arrived.shape[1:], f32)

    barrier = pltpu.get_barrier_semaphore()
    for step in range(1, count_z):
        pl.semaphore_signal(barrier, inc=1, device_id=z_partner(step), device_id_type=MESH)
    for step in range(1, count_x * count_y):
        pl.semaphore_signal(barrier, inc=1, device_id=xy_partner(step), device_id_type=MESH)
    pl.semaphore_wait(barrier, count_z - 1 + count_x * count_y - 1)
    for copy in bring:
        copy.wait()

    def exchange(slot, down, up, down_id, up_id, has_down, has_up):
        to_down = pltpu.make_async_remote_copy(
            src_ref=down[0], dst_ref=down[1], send_sem=face_send.at[slot],
            recv_sem=face_recv.at[slot], device_id=down_id, device_id_type=MESH,
        )
        to_up = pltpu.make_async_remote_copy(
            src_ref=up[0], dst_ref=up[1], send_sem=face_send.at[slot + 1],
            recv_sem=face_recv.at[slot + 1], device_id=up_id, device_id_type=MESH,
        )

        @pl.when(has_down)
        def _():
            to_down.start()

        @pl.when(has_up)
        def _():
            to_up.start()

        def finish():
            @pl.when(has_up)
            def _():
                to_down.wait_recv()
                to_up.wait_send()

            @pl.when(has_down)
            def _():
                to_up.wait_recv()
                to_down.wait_send()

        return finish

    main = pl.ds(0, size_z)
    every = pl.ds(0, rows)

    def exchange_y(slot, which, wide):
        return exchange(
            slot,
            (
                field.at[which, inner, pl.ds(0, wide), main],
                field.at[which, inner, pl.ds(size_y, wide), main],
            ),
            (
                field.at[which, inner, pl.ds(size_y - wide, wide), main],
                field.at[which, inner, pl.ds(rows - wide, wide), main],
            ),
            (ix, lax.max(iy - 1, 0), iz),
            (ix, lax.min(iy + 1, count_y - 1), iz),
            iy > 0,
            iy < count_y - 1,
        )

    def exchange_x(slot, which, low, high):
        return exchange(
            slot,
            (
                field.at[which, pl.ds(HALO, high), every, main],
                field.at[which, pl.ds(HALO + size_x, high), every, main],
            ),
            (
                field.at[which, pl.ds(HALO + size_x - low, low), every, main],
                field.at[which, pl.ds(HALO - low, low), every, main],
            ),
            (lax.max(ix - 1, 0), iy, iz),
            (lax.min(ix + 1, count_x - 1), iy, iz),
            ix > 0,
            ix < count_x - 1,
        )

    def exchange_z(slot, which):
        return exchange(
            slot,
            (packed.at[which], arrived.at[0, which]),
            (packed.at[which], arrived.at[1, which]),
            (ix, iy, lax.max(iz - 1, 0)),
            (ix, iy, lax.min(iz + 1, count_z - 1)),
            iz > 0,
            iz < count_z - 1,
        )

    lane_of = lax.broadcasted_iota(jnp.int32, (PAD, LANES), 1)
    in_group = lax.rem(lane_of, group)

    def pack(indices):
        def body(chunk):
            for plane, index in itertools.product(chunk, indices):
                out = jnp.zeros((PAD, LANES), f32)
                for tile in range(count_t):
                    at = tile * group
                    mine = field[index, plane, tile * PAD : (tile + 1) * PAD]
                    here = (lane_of >= at + PAD) & (lane_of < at + 2 * PAD)
                    out = jnp.where(here, roll(mine, at + PAD), out)
                    here = (lane_of >= at + 2 * PAD) & (lane_of < at + 3 * PAD)
                    out = jnp.where(here, roll(mine, at + 3 * PAD), out)
                packed[index, plane] = out

        return body

    def unpack(indices):
        def body(chunk):
            for plane, index in itertools.product(chunk, indices):
                below = roll(arrived[1, index, plane], -2 * PAD)
                above = roll(arrived[0, index, plane], 2 * PAD)
                value = jnp.where(in_group < PAD, below, packed[index, plane])
                field[index, plane, rows:] = jnp.where(in_group >= 3 * PAD, above, value)

        return body

    some = planes // 2
    one, three = pl.ds(0, 1), pl.ds(1, 3)
    design_y = exchange_y(0, one, PAD)
    load_y = exchange_y(2, three, 4)
    design_y()
    design_x = exchange_x(4, one, HALO, HALO)

    row_at = lax.broadcasted_iota(jnp.int32, (rows, lanes), 0)
    lane_at = lax.broadcasted_iota(jnp.int32, (rows, lanes), 1)
    edge_row = lax.broadcasted_iota(jnp.int32, (PAD, lanes), 0) + lane_of // group * PAD
    edge_lane = jnp.where(in_group < 2 * PAD, in_group - PAD, in_group + size_z - 3 * PAD)
    row_at = jnp.concatenate([row_at, edge_row], 0)
    lane_at = jnp.concatenate([lane_at, edge_lane], 0) + iz * size_z
    row_at = jnp.where(row_at < size_y + PAD, row_at, row_at - rows) + iy * size_y
    inside_yz = (
        (row_at >= 0) & (row_at < size_y * count_y) & (lane_at >= 0) & (lane_at < size_z * count_z)
    )
    masks[0] = jnp.where(inside_yz, 1.0, 0.0).astype(f32)
    for far_x, tiles in enumerate(zip(*cone_tiles(table, tiles_of(masks[0]), range(count_t + 1)))):
        value = jnp.concatenate(tiles, 0)
        masks[1 + far_x, :rows] = patched(value, count_t)
        masks[1 + far_x, rows:] = value[rows:]

    def inside_x(plane):
        where = plane + ix * size_x
        return jnp.where((where >= 0) & (where < size_x * count_x), 1.0, 0.0).astype(f32)

    bricks_x, bricks_y, bricks_z = size_x // BRICK, size_y // BRICK, size_z // BRICK

    def brick(bx, by, bz):
        gx, gy, gz = ix * bricks_x + bx, iy * bricks_y + by, iz * bricks_z + bz
        top_x, top_y, top_z = bricks_x * count_x, bricks_y * count_y, bricks_z * count_z
        good = (gx >= 0) & (gx < top_x) & (gy >= 0) & (gy < top_y) & (gz >= 0) & (gz < top_z)
        value = solid[
            lax.clamp(0, gx, top_x - 1), lax.clamp(0, gy, top_y - 1), lax.clamp(0, gz, top_z - 1)
        ]
        return value.astype(f32) * jnp.where(good, 1.0, 0.0).astype(f32)

    for bx in range(-1, bricks_x + 1):
        edge = jnp.zeros((PAD, lanes), f32)
        for by in range(-1, bricks_y + 1):
            line = jnp.zeros((PAD, lanes), f32)
            for bz in range(bricks_z):
                here = (lane_of >= bz * BRICK) & (lane_of < (bz + 1) * BRICK)
                line = jnp.where(here, brick(bx, by, bz), line)
            if by < 0:
                spots = [size_y + PAD]
            elif by == bricks_y:
                spots = [size_y]
            else:
                spots = range(by * BRICK, (by + 1) * BRICK, PAD)
            around = jnp.zeros((PAD, lanes), f32)
            for part, bz in enumerate((-1, 0, bricks_z - 1, bricks_z)):
                around = jnp.where(in_group >= part * PAD, brick(bx, by, bz), around)
            for spot in spots:
                flags[bx + 1, spot : spot + PAD, :] = line
                edge = jnp.where(lane_of // group == spot // PAD, around, edge)
        flags[bx + 1, rows:, :] = edge

    design_x()
    in_chunks(0, 2, some, pack((0,)))
    design_z = exchange_z(6, one)
    load_y()
    load_x = exchange_x(8, three, 3, 4)
    design_z()
    in_chunks(0, 2, some, unpack((0,)))

    begin = jnp.where(first, 2, 0)
    at_side = first | last

    all_tiles = range(count_t + 1)
    own_tiles = (*range(size_y // PAD), count_t)

    def filter_planes(chunk):
        for plane in chunk:
            for at, sums in enumerate(cone_tiles(table, tiles_of(field[0, plane]), all_tiles)):
                for far_x in range(3):
                    cone[far_x, plane, at * PAD : (at + 1) * PAD] = sums[far_x]

    in_chunks(begin, jnp.where(at_side, (planes + 1) // 4, (planes + 3) // 4), 4, filter_planes)
    lift = math.tanh(sharpness * threshold)
    scale = lift + math.tanh(sharpness * (1.0 - threshold))

    def gathered(source, plane):
        return (
            source[0, plane]
            + (source[1, plane - 1] + source[1, plane + 1])
            + (source[2, plane - 2] + source[2, plane + 2])
        )

    load_x()
    in_chunks(0, some, 2, pack((1, 2, 3)))
    load_z = exchange_z(10, three)

    def material(chunk):
        for step in chunk:
            at = step - 3
            plane = step + 2
            weight = inside_x(at) * masks[1]
            weight = weight + (inside_x(at - 1) + inside_x(at + 1)) * masks[2]
            weight = weight + (inside_x(at - 2) + inside_x(at + 2)) * masks[3]
            weight = 1.0 / jnp.maximum(weight, 1.0)
            smoothed = gathered(cone, plane)
            smoothed = jnp.concatenate([patched(smoothed, count_t), smoothed[rows:]], 0)
            tanh_shift = jnp.tanh(sharpness * (smoothed * weight - threshold))
            density = (lift + tanh_shift) * (1.0 / scale)
            flag = flags[(at + BRICK) // BRICK]
            squared = density * density
            moduli[step] = (young_floor + (1.0 - young_floor) * (squared * density)) * flag
            slope = (1.0 - tanh_shift * tanh_shift) * weight
            factor[step] = (
                (-3.0 * (1.0 - young_floor) * sharpness / scale) * (squared * flag) * slope
            )

            @pl.when((at >= 0) & (at < size_x))
            def _():
                dens_out[lax.clamp(0, at, size_x - 1)] = density[:size_y]

    chunks = jnp.where(at_side, (size_x + 6) // 4, (size_x + 9) // 4)
    in_chunks(begin, chunks, 4, material)
    load_z()
    in_chunks(0, some, 2, unpack((1, 2, 3)))

    def start(values, chosen):
        parts = z_parts(values)
        for at in chosen:
            modes = tile_modes(parts, at)
            for number, key in enumerate(KEYS):
                held[number, at * PAD : (at + 1) * PAD] = modes[key]

    start([field[comp + 1, begin + 2] for comp in range(3)], all_tiles)
    carry[...] = jnp.zeros_like(carry)

    def operate(chunk):
        parts = [z_parts([field[comp + 1, step + 3] for comp in range(3)]) for step in chunk]
        moved = [{} for _ in chunk]
        stays = [{} for _ in chunk]
        for at in all_tiles:
            spot = slice(at * PAD, (at + 1) * PAD)
            old = {key: held[number, spot] for number, key in enumerate(KEYS)}
            above = {key: carry[number, spot] for number, key in enumerate(KEYS)}
            for place, step in enumerate(chunk):
                new = tile_modes(parts[place], at)
                forces = modal_product(modal, element_modes(old, new))
                old = new
                stiff = moduli[step, spot]
                at_node = {}
                for key in KEYS:
                    even, odd = forces[key_row(0, key)], forces[key_row(1, key)]
                    odd = odd * stiff
                    if even is None:
                        at_node[key] = above[key] - odd
                        above[key] = odd
                    else:
                        even = even * stiff
                        at_node[key] = above[key] + (even - odd)
                        above[key] = even + odd
                for comp, mode_z in itertools.product(range(3), range(2)):
                    even, odd = at_node[(comp, 0, mode_z)], at_node[(comp, 1, mode_z)]
                    moved[place].setdefault((comp, mode_z), []).append(even + odd)
                    stays[place].setdefault((comp, mode_z), []).append(even - odd)
            for number, key in enumerate(KEYS):
                held[number, spot] = old[key]
                carry[number, spot] = above[key]
        for place, step in enumerate(chunk):
            known = inside_x(step - 3)
            for comp in range(3):
                totals = []
                for at in all_tiles:
                    spot = slice(at * PAD, (at + 1) * PAD)
                    along = [
                        stays[place][(comp, mode_z)][at]
                        + shift_tile(moved[place][(comp, mode_z)], at, 1)
                        for mode_z in range(2)
                    ]
                    total = (along[0] - along[1]) + roll(along[0] + along[1], 1)
                    total = total + spring_rate * field[comp + 1, step + 2, spot]
                    totals.append(total * (masks[0, spot] * known))
                total = jnp.concatenate(totals, 0)
                applied[comp, step, :rows] = patched(total, count_t)
                applied[comp, step, rows:] = totals[-1]

    in_chunks(begin, chunks, 4, operate)

    start([applied[comp, 3] for comp in range(3)], own_tiles)

    def products(number, sums):
        rr, rs, ss, es = sums
        chunk = [number * 4 + at for at in range(4)]
        parts = [z_parts([applied[comp, step + 4] for comp in range(3)]) for step in chunk]
        for step, comp in itertools.product(chunk, range(3)):
            res = field[comp + 1, step + HALO, :size_y]
            app = applied[comp, step + 3, :size_y]
            rr, rs, ss = rr + res * res, rs + res * app, ss + app * app
        strain = tiles_of(es)
        for number, at in enumerate(own_tiles):
            spot = slice(at * PAD, (at + 1) * PAD)
            old = {key: held[number, spot] for number, key in enumerate(KEYS)}
            for place, step in enumerate(chunk):
                new = tile_modes(parts[place], at)
                energy = modal_energy(modal, element_modes(old, new))
                old = new
                strain[number] = strain[number] + energy * moduli[step + 3, spot]
            for key_number, key in enumerate(KEYS):
                held[key_number, spot] = old[key]
        return rr, rs, ss, jnp.concatenate(strain, 0)

    nothing = jnp.zeros((size_y, size_z), f32)
    most = jnp.zeros((size_y + PAD, size_z), f32)
    sums = list(lax.fori_loop(0, size_x // 4, products, (nothing, nothing, nothing, most)))
    lane_main = lax.broadcasted_iota(jnp.int32, (size_y, lanes), 1)
    strain = jnp.where(lane_main < size_z - 1, sums[3][:size_y], 0.0)
    ends = (in_group == 3 * PAD - 1) & (lane_of < size_y // PAD * group)
    sums[3] = jnp.concatenate([strain, jnp.where(ends, sums[3][size_y:], 0.0)], 0)
    row8 = lax.broadcasted_iota(jnp.int32, (8, LANES), 0)
    tile = jnp.zeros((8, LANES), f32)
    for number, value in enumerate(sums):
        line = jnp.sum(value, axis=0, keepdims=True)
        tile = jnp.where(row8 == number, line, tile)

    def all_sum(slots, partner, count, send, recv):
        copies = [
            pltpu.make_async_remote_copy(
                src_ref=slots.at[0], dst_ref=slots.at[step], send_sem=send.at[step],
                recv_sem=recv.at[step], device_id=partner(step), device_id_type=MESH,
            )
            for step in range(1, count)
        ]
        for copy in copies:
            copy.start()
        total = slots[0]
        for step, copy in enumerate(copies):
            copy.wait_recv()
            total = total + slots[step + 1]
        for copy in copies:
            copy.wait_send()
        return total

    part_z[0] = tile
    part_xy[0] = all_sum(part_z, z_partner, count_z, z_send, z_recv)
    total = all_sum(part_xy, xy_partner, count_x * count_y, xy_send, xy_recv)
    total = jnp.sum(total, axis=1, keepdims=True)
    rr, rs, ss, es = (total[number : number + 1] for number in range(4))
    st = es + spring_rate * ss
    step_first = rr / rs
    rr_next = step_first * step_first * ss - rr
    product = rs - 2.0 * step_first * ss + step_first * step_first * st
    ratio = rr_next / rr
    step_second = rr_next / (product - ratio * rr_next / step_first)
    by_load = step_first + step_second * (1.0 + ratio)
    by_applied = -step_first * step_second

    def displaced(comp, plane):
        return by_load * field[comp + 1, plane + 2] + by_applied * applied[comp, plane]

    for far_x in range(3):
        for side, spot in ((first, 0), (last, size_x + 2)):

            @pl.when(side)
            def _():
                pushed[far_x, spot : spot + 2] = jnp.zeros((2, size_y + PAD, size_z), f32)

    start([displaced(comp, begin + 1) for comp in range(3)], all_tiles)

    def energies(chunk):
        parts = [z_parts([displaced(comp, step + 2) for comp in range(3)]) for step in chunk]
        pushes = [[] for _ in chunk]
        for at in all_tiles:
            spot = slice(at * PAD, (at + 1) * PAD)
            old = {key: held[number, spot] for number, key in enumerate(KEYS)}
            for place, step in enumerate(chunk):
                new = tile_modes(parts[place], at)
                energy = modal_energy(modal, element_modes(old, new))
                old = new
                pushes[place].append(energy * factor[step + 1, spot])
            for number, key in enumerate(KEYS):
                held[number, spot] = old[key]
        for place, step in enumerate(chunk):
            for number, sums in enumerate(cone_tiles(table, pushes[place], own_tiles)):
                for far_x in range(3):
                    pushed[far_x, step, number * PAD : (number + 1) * PAD] = sums[far_x]

    in_chunks(begin, jnp.where(at_side, (size_x + 7) // 6, (size_x + 9) // 6), 6, energies)

    def finish(chunk):
        for plane in chunk:
            sens_out[plane] = patched(gathered(pushed, plane + 2), count_t)
            for comp in range(3):
                disp_out[comp, plane] = displaced(comp, plane + 3)[:size_y]

    in_chunks(0, size_x // 4, 4, finish)


def solution(mesh):
    counts = tuple(mesh.shape[name] for name in ("gx", "gy", "gz"))
    placed = (P(None, "gx", "gy", "gz"), P("gx", "gy", "gz"), P())

    def body(load_field, design, solid_map):
        size_x, size_y, size_z = design.shape
        rows = size_y + 2 * PAD
        full, lanes = rows + PAD, size_z
        planes = size_x + 2 * HALO
        f32 = jnp.float32
        vmem = pl.BlockSpec(memory_space=pltpu.VMEM)
        anywhere = pl.BlockSpec(memory_space=pltpu.HBM)
        pairs = counts[0] * counts[1]
        dma = pltpu.SemaphoreType.DMA

        def run(*refs):
            kernel(counts, *refs)

        return pl.pallas_call(
            run,
            out_shape=(
                jax.ShapeDtypeStruct(load_field.shape, f32),
                jax.ShapeDtypeStruct(design.shape, f32),
                jax.ShapeDtypeStruct(design.shape, f32),
            ),
            in_specs=[anywhere, anywhere, pl.BlockSpec(memory_space=pltpu.SMEM)],
            out_specs=(vmem, vmem, vmem),
            scratch_shapes=[
                pltpu.VMEM((4, planes + 2, full, lanes), f32),
                pltpu.VMEM((3, size_x + 10, full, lanes), f32),
                pltpu.VMEM((size_x + 10, full, lanes), f32),
                pltpu.VMEM((size_x + 10, full, lanes), f32),
                pltpu.VMEM((size_x // BRICK + 2, full, lanes), f32),
                pltpu.VMEM((3, planes + 6, full, lanes), f32),
                pltpu.VMEM((3, size_x + 8, size_y + PAD, size_z), f32),
                pltpu.VMEM((12, full, lanes), f32),
                pltpu.VMEM((12, full, lanes), f32),
                pltpu.VMEM((4, planes, PAD, LANES), f32),
                pltpu.VMEM((2, 4, planes, PAD, LANES), f32),
                pltpu.VMEM((4, full, lanes), f32),
                pltpu.VMEM((counts[2], 8, LANES), f32),
                pltpu.VMEM((pairs, 8, LANES), f32),
                dma((12,)),
                dma((12,)),
                dma((counts[2],)),
                dma((counts[2],)),
                dma((pairs,)),
                dma((pairs,)),
                dma((4,)),
            ],
            compiler_params=pltpu.CompilerParams(
                collective_id=0, has_side_effects=True, vmem_limit_bytes=40 * 2**20
            ),
        )(load_field, design, solid_map)

    return jax.shard_map(
        body,
        mesh=mesh,
        in_specs=placed,
        out_specs=(P(None, "gx", "gy", "gz"), P("gx", "gy", "gz"), P("gx", "gy", "gz")),
        check_vma=False,
    )
```

```python
import itertools
import math

import jax
import jax.numpy as jnp
import numpy as np
from jax import lax
from jax.experimental import pallas as pl
from jax.experimental.pallas import tpu as pltpu
from jax.sharding import PartitionSpec as P

BRICK = 16
HALO = 5
PAD = 8
LANES = 128

young_floor = 0.001
spring_rate = 0.05
sharpness = 8.0
threshold = 0.5
poisson = 0.3
MESH = pl.DeviceIdType.MESH


def element_matrix():
    lame_first = poisson / ((1.0 + poisson) * (1.0 - 2.0 * poisson))
    shear_mod = 1.0 / (2.0 * (1.0 + poisson))
    elastic = np.zeros((6, 6))
    elastic[:3, :3] = lame_first
    for axis_one in range(3):
        elastic[axis_one, axis_one] += 2.0 * shear_mod
        elastic[axis_one + 3, axis_one + 3] = shear_mod
    gauss_point = 1.0 / math.sqrt(3.0)
    stiffness = np.zeros((24, 24))
    for point_x in (-gauss_point, gauss_point):
        for point_y in (-gauss_point, gauss_point):
            for point_z in (-gauss_point, gauss_point):
                strain = np.zeros((6, 24))
                for corner in range(8):
                    sign_a = 2 * (corner // 4) - 1
                    sign_b = 2 * (corner // 2 % 2) - 1
                    sign_c = 2 * (corner % 2) - 1
                    along_x = 0.25 * sign_a * (1 + sign_b * point_y) * (1 + sign_c * point_z)
                    along_y = 0.25 * (1 + sign_a * point_x) * sign_b * (1 + sign_c * point_z)
                    along_z = 0.25 * (1 + sign_a * point_x) * (1 + sign_b * point_y) * sign_c
                    column = 3 * corner
                    strain[0, column] = along_x
                    strain[1, column + 1] = along_y
                    strain[2, column + 2] = along_z
                    strain[3, column + 1] = along_z
                    strain[3, column + 2] = along_y
                    strain[4, column] = along_z
                    strain[4, column + 2] = along_x
                    strain[5, column] = along_y
                    strain[5, column + 1] = along_x
                stiffness += strain.T @ elastic @ strain * 0.125
    return stiffness


def cone_offsets():
    listed = []
    for step_x in range(-2, 3):
        for step_y in range(-2, 3):
            for step_z in range(-2, 3):
                radius = step_x * step_x + step_y * step_y + step_z * step_z
                if radius < 9:
                    listed.append((step_x, step_y, step_z, 3.0 - math.sqrt(radius)))
    return listed


def modal_matrix():
    stiffness = element_matrix()
    change = np.zeros((24, 24))
    for mode in itertools.product((0, 1), repeat=3):
        for corner in itertools.product((0, 1), repeat=3):
            sign = 1.0
            for is_diff, side in zip(mode, corner):
                sign *= (2 * side - 1) if is_diff else 1
            for comp in range(3):
                row = 3 * (4 * mode[0] + 2 * mode[1] + mode[2]) + comp
                change[row, 3 * (4 * corner[0] + 2 * corner[1] + corner[2]) + comp] = sign
    modal = change @ stiffness @ change.T / 64.0
    modal[np.abs(modal) < 1e-10] = 0.0
    return modal


def cone_table():
    table = {}
    for step_x, step_y, step_z, weight in cone_offsets():
        if min(step_x, step_y, step_z) >= 0:
            table[(step_x, step_y, step_z)] = weight
    return table


MODES = tuple(itertools.product((0, 1), repeat=2))


def roll(value, shift):
    return pltpu.roll(value, shift % value.shape[1], 1)


def tiles_of(value):
    return [value[at : at + PAD] for at in range(0, value.shape[0], PAD)]


def shift_tile(tiles, at, shift):
    count = len(tiles) - 1
    if at == count:
        group = LANES // count
        other = roll(tiles[at], group if shift > 0 else -group)
    else:
        other = tiles[(at - 1) % count] if shift > 0 else tiles[(at + 1) % count]
    row = lax.broadcasted_iota(jnp.int32, (PAD, LANES), 0)
    far = row >= PAD - shift if shift > 0 else row < -shift
    return pltpu.roll(jnp.where(far, other, tiles[at]), shift % PAD, 0)


def z_parts(values):
    out = {}
    for comp, value in enumerate(values):
        tiles = tiles_of(value)
        ahead = [roll(tile, -1) for tile in tiles]
        out[(comp, 0)] = [tile + other for tile, other in zip(tiles, ahead)]
        out[(comp, 1)] = [other - tile for tile, other in zip(tiles, ahead)]
    return out


def tile_modes(parts, at):
    out = {}
    for (comp, mode_z), tiles in parts.items():
        above = shift_tile(tiles, at, -1)
        out[(comp, 0, mode_z)] = tiles[at] + above
        out[(comp, 1, mode_z)] = above - tiles[at]
    return out


def patched(value, count):
    edge = value[-PAD:]
    height = value.shape[0] - PAD
    group = LANES // count
    lane = lax.broadcasted_iota(jnp.int32, edge.shape, 1)
    out = []
    for tile in range(height // PAD):
        low = roll(edge, -(tile * group + PAD))
        high = roll(edge, LANES - 3 * PAD - tile * group)
        mine = jnp.where(lane < 2, low, value[tile * PAD : (tile + 1) * PAD])
        out.append(jnp.where(lane >= LANES - 3, high, mine))
    return jnp.concatenate(out, 0)


def modal_product(modal, modes):
    out = {}
    for row in range(24):
        total = None
        for col in range(24):
            if modal[row, col] != 0.0:
                term = modes[col] * float(modal[row, col])
                total = term if total is None else total + term
        out[row] = total
    return out


def key_row(mode_x, key):
    comp, mode_y, mode_z = key
    return 3 * (4 * mode_x + 2 * mode_y + mode_z) + comp


KEYS = tuple((comp, my, mz) for comp in range(3) for my, mz in MODES)


def element_modes(old, new):
    modes = {}
    for key in KEYS:
        modes[key_row(0, key)] = old[key] + new[key]
        modes[key_row(1, key)] = new[key] - old[key]
    return modes


def modal_energy(modal, modes):
    forces = modal_product(modal, modes)
    total = None
    for row in range(24):
        if forces[row] is not None:
            term = forces[row] * modes[row]
            total = term if total is None else total + term
    return total


def cone_tiles(table, tiles, chosen):
    along_z = (
        tiles,
        [roll(tile, 1) + roll(tile, -1) for tile in tiles],
        [roll(tile, 2) + roll(tile, -2) for tile in tiles],
    )
    out = []
    for at in chosen:
        sums = [None, None, None]
        for far_z, part in enumerate(along_z):
            along_y = (
                part[at],
                shift_tile(part, at, 1) + shift_tile(part, at, -1),
                shift_tile(part, at, 2) + shift_tile(part, at, -2),
            )
            for far_x in range(3):
                for far_y in range(3):
                    weight = table.get((far_x, far_y, far_z))
                    if weight is not None:
                        term = along_y[far_y] * weight
                        sums[far_x] = term if sums[far_x] is None else sums[far_x] + term
        out.append(sums)
    return out


def in_chunks(begin, chunks, size, body):
    def step(number, _):
        body([begin + number * size + at for at in range(size)])
        return 0

    lax.fori_loop(0, chunks, step, 0)


def kernel(
    counts,
    load,
    design,
    solid,
    disp_out,
    sens_out,
    dens_out,
    field,
    applied,
    moduli,
    factor,
    flags,
    cone,
    pushed,
    held,
    carry,
    packed,
    arrived,
    masks,
    part_z,
    part_xy,
    face_send,
    face_recv,
    z_send,
    z_recv,
    xy_send,
    xy_recv,
    copy_sem,
):
    count_x, count_y, count_z = counts
    size_x, size_y, size_z = design.shape
    rows = size_y + 2 * PAD
    full, lanes = rows + PAD, size_z
    count_t = rows // PAD
    group = LANES // count_t
    planes = size_x + 2 * HALO
    first, last = lax.axis_index("gx") == 0, lax.axis_index("gx") == count_x - 1
    ix, iy, iz = lax.axis_index("gx"), lax.axis_index("gy"), lax.axis_index("gz")
    modal = modal_matrix()
    table = cone_table()
    f32 = jnp.float32

    def z_partner(step):
        return (ix, iy, lax.rem(iz + step, count_z))

    def xy_partner(step):
        spot = lax.rem(ix * count_y + iy + step, count_x * count_y)
        return (spot // count_y, lax.rem(spot, count_y), iz)

    inner = pl.ds(HALO, size_x)
    bring = [pltpu.make_async_copy(design, field.at[0, inner, pl.ds(0, size_y)], copy_sem.at[0])]
    for comp in range(3):
        bring.append(
            pltpu.make_async_copy(
                load.at[comp], field.at[comp + 1, inner, pl.ds(0, size_y)], copy_sem.at[comp + 1]
            )
        )
    for copy in bring:
        copy.start()

    for index in range(4):

        def clear(plane, _):
            field[index, plane + HALO, size_y:rows] = jnp.zeros((rows - size_y, lanes), f32)
            return 0

        lax.fori_loop(0, size_x, clear, 0)
        for plane in range(HALO):
            field[index, plane, :rows] = jnp.zeros((rows, lanes), f32)
            field[index, plane + HALO + size_x, :rows] = jnp.zeros((rows, lanes), f32)

    @pl.when(iz == 0)
    def _():
        arrived[1] = jnp.zeros(arrived.shape[1:], f32)

    @pl.when(iz == count_z - 1)
    def _():
        arrived[0] = jnp.zeros(arrived.shape[1:], f32)

    barrier = pltpu.get_barrier_semaphore()
    for step in range(1, count_z):
        pl.semaphore_signal(barrier, inc=1, device_id=z_partner(step), device_id_type=MESH)
    for step in range(1, count_x * count_y):
        pl.semaphore_signal(barrier, inc=1, device_id=xy_partner(step), device_id_type=MESH)
    pl.semaphore_wait(barrier, count_z - 1 + count_x * count_y - 1)
    for copy in bring:
        copy.wait()

    def exchange(slot, down, up, down_id, up_id, has_down, has_up):
        to_down = pltpu.make_async_remote_copy(
            src_ref=down[0], dst_ref=down[1], send_sem=face_send.at[slot],
            recv_sem=face_recv.at[slot], device_id=down_id, device_id_type=MESH,
        )
        to_up = pltpu.make_async_remote_copy(
            src_ref=up[0], dst_ref=up[1], send_sem=face_send.at[slot + 1],
            recv_sem=face_recv.at[slot + 1], device_id=up_id, device_id_type=MESH,
        )

        @pl.when(has_down)
        def _():
            to_down.start()

        @pl.when(has_up)
        def _():
            to_up.start()

        def finish():
            @pl.when(has_up)
            def _():
                to_down.wait_recv()
                to_up.wait_send()

            @pl.when(has_down)
            def _():
                to_up.wait_recv()
                to_down.wait_send()

        return finish

    main = pl.ds(0, size_z)
    every = pl.ds(0, rows)

    def exchange_y(slot, which, wide):
        return exchange(
            slot,
            (
                field.at[which, inner, pl.ds(0, wide), main],
                field.at[which, inner, pl.ds(size_y, wide), main],
            ),
            (
                field.at[which, inner, pl.ds(size_y - wide, wide), main],
                field.at[which, inner, pl.ds(rows - wide, wide), main],
            ),
            (ix, lax.max(iy - 1, 0), iz),
            (ix, lax.min(iy + 1, count_y - 1), iz),
            iy > 0,
            iy < count_y - 1,
        )

    def exchange_x(slot, which, low, high):
        return exchange(
            slot,
            (
                field.at[which, pl.ds(HALO, high), every, main],
                field.at[which, pl.ds(HALO + size_x, high), every, main],
            ),
            (
                field.at[which, pl.ds(HALO + size_x - low, low), every, main],
                field.at[which, pl.ds(HALO - low, low), every, main],
            ),
            (lax.max(ix - 1, 0), iy, iz),
            (lax.min(ix + 1, count_x - 1), iy, iz),
            ix > 0,
            ix < count_x - 1,
        )

    def exchange_z(slot, which):
        return exchange(
            slot,
            (packed.at[which], arrived.at[0, which]),
            (packed.at[which], arrived.at[1, which]),
            (ix, iy, lax.max(iz - 1, 0)),
            (ix, iy, lax.min(iz + 1, count_z - 1)),
            iz > 0,
            iz < count_z - 1,
        )

    lane_of = lax.broadcasted_iota(jnp.int32, (PAD, LANES), 1)
    in_group = lax.rem(lane_of, group)

    def pack(indices):
        def body(chunk):
            for plane, index in itertools.product(chunk, indices):
                out = jnp.zeros((PAD, LANES), f32)
                for tile in range(count_t):
                    at = tile * group
                    mine = field[index, plane, tile * PAD : (tile + 1) * PAD]
                    here = (lane_of >= at + PAD) & (lane_of < at + 2 * PAD)
                    out = jnp.where(here, roll(mine, at + PAD), out)
                    here = (lane_of >= at + 2 * PAD) & (lane_of < at + 3 * PAD)
                    out = jnp.where(here, roll(mine, at + 3 * PAD), out)
                packed[index, plane] = out

        return body

    def unpack(indices):
        def body(chunk):
            for plane, index in itertools.product(chunk, indices):
                below = roll(arrived[1, index, plane], -2 * PAD)
                above = roll(arrived[0, index, plane], 2 * PAD)
                value = jnp.where(in_group < PAD, below, packed[index, plane])
                field[index, plane, rows:] = jnp.where(in_group >= 3 * PAD, above, value)

        return body

    some = planes // 2
    one, three = pl.ds(0, 1), pl.ds(1, 3)
    design_y = exchange_y(0, one, HALO)
    design_y()
    design_x = exchange_x(4, one, HALO, HALO)
    load_y = exchange_y(2, three, 4)

    row_at = lax.broadcasted_iota(jnp.int32, (rows, lanes), 0)
    lane_at = lax.broadcasted_iota(jnp.int32, (rows, lanes), 1)
    edge_row = lax.broadcasted_iota(jnp.int32, (PAD, lanes), 0) + lane_of // group * PAD
    edge_lane = jnp.where(in_group < 2 * PAD, in_group - PAD, in_group + size_z - 3 * PAD)
    row_at = jnp.concatenate([row_at, edge_row], 0)
    lane_at = jnp.concatenate([lane_at, edge_lane], 0) + iz * size_z
    row_at = jnp.where(row_at < size_y + PAD, row_at, row_at - rows) + iy * size_y
    inside_yz = (
        (row_at >= 0) & (row_at < size_y * count_y) & (lane_at >= 0) & (lane_at < size_z * count_z)
    )
    masks[0] = jnp.where(inside_yz, 1.0, 0.0).astype(f32)
    for far_x, tiles in enumerate(zip(*cone_tiles(table, tiles_of(masks[0]), range(count_t + 1)))):
        value = jnp.concatenate(tiles, 0)
        masks[1 + far_x, :rows] = patched(value, count_t)
        masks[1 + far_x, rows:] = value[rows:]

    def inside_x(plane):
        where = plane + ix * size_x
        return jnp.where((where >= 0) & (where < size_x * count_x), 1.0, 0.0).astype(f32)

    bricks_x, bricks_y, bricks_z = size_x // BRICK, size_y // BRICK, size_z // BRICK

    def brick(bx, by, bz):
        gx, gy, gz = ix * bricks_x + bx, iy * bricks_y + by, iz * bricks_z + bz
        top_x, top_y, top_z = bricks_x * count_x, bricks_y * count_y, bricks_z * count_z
        good = (gx >= 0) & (gx < top_x) & (gy >= 0) & (gy < top_y) & (gz >= 0) & (gz < top_z)
        value = solid[
            lax.clamp(0, gx, top_x - 1), lax.clamp(0, gy, top_y - 1), lax.clamp(0, gz, top_z - 1)
        ]
        return value.astype(f32) * jnp.where(good, 1.0, 0.0).astype(f32)

    for bx in range(-1, bricks_x + 1):
        edge = jnp.zeros((PAD, lanes), f32)
        for by in range(-1, bricks_y + 1):
            line = jnp.zeros((PAD, lanes), f32)
            for bz in range(bricks_z):
                here = (lane_of >= bz * BRICK) & (lane_of < (bz + 1) * BRICK)
                line = jnp.where(here, brick(bx, by, bz), line)
            if by < 0:
                spots = [size_y + PAD]
            elif by == bricks_y:
                spots = [size_y]
            else:
                spots = range(by * BRICK, (by + 1) * BRICK, PAD)
            around = jnp.zeros((PAD, lanes), f32)
            for part, bz in enumerate((-1, 0, bricks_z - 1, bricks_z)):
                around = jnp.where(in_group >= part * PAD, brick(bx, by, bz), around)
            for spot in spots:
                flags[bx + 1, spot : spot + PAD, :] = line
                edge = jnp.where(lane_of // group == spot // PAD, around, edge)
        flags[bx + 1, rows:, :] = edge

    design_x()
    in_chunks(0, 2, some, pack((0,)))
    design_z = exchange_z(6, one)
    load_y()
    load_x = exchange_x(8, three, 3, 4)
    design_z()
    in_chunks(0, 2, some, unpack((0,)))

    begin = jnp.where(first, 2, 0)
    at_side = first | last

    all_tiles = range(count_t + 1)
    own_tiles = (*range(size_y // PAD), count_t)

    def filter_planes(chunk):
        for plane in chunk:
            for at, sums in enumerate(cone_tiles(table, tiles_of(field[0, plane]), all_tiles)):
                for far_x in range(3):
                    cone[far_x, plane, at * PAD : (at + 1) * PAD] = sums[far_x]

    in_chunks(begin, jnp.where(at_side, (planes + 1) // 4, (planes + 3) // 4), 4, filter_planes)
    lift = math.tanh(sharpness * threshold)
    scale = lift + math.tanh(sharpness * (1.0 - threshold))

    def gathered(source, plane):
        return (
            source[0, plane]
            + (source[1, plane - 1] + source[1, plane + 1])
            + (source[2, plane - 2] + source[2, plane + 2])
        )

    load_x()
    in_chunks(0, some, 2, pack((1, 2, 3)))
    load_z = exchange_z(10, three)

    def material(chunk):
        for step in chunk:
            at = step - 3
            plane = step + 2
            weight = inside_x(at) * masks[1]
            weight = weight + (inside_x(at - 1) + inside_x(at + 1)) * masks[2]
            weight = weight + (inside_x(at - 2) + inside_x(at + 2)) * masks[3]
            weight = 1.0 / jnp.maximum(weight, 1.0)
            smoothed = gathered(cone, plane)
            smoothed = jnp.concatenate([patched(smoothed, count_t), smoothed[rows:]], 0)
            tanh_shift = jnp.tanh(sharpness * (smoothed * weight - threshold))
            density = (lift + tanh_shift) * (1.0 / scale)
            flag = flags[(at + BRICK) // BRICK]
            squared = density * density
            moduli[step] = (young_floor + (1.0 - young_floor) * (squared * density)) * flag
            slope = (1.0 - tanh_shift * tanh_shift) * weight
            factor[step] = (
                (-3.0 * (1.0 - young_floor) * sharpness / scale) * (squared * flag) * slope
            )

            @pl.when((at >= 0) & (at < size_x))
            def _():
                dens_out[lax.clamp(0, at, size_x - 1)] = density[:size_y]

    chunks = jnp.where(at_side, (size_x + 6) // 4, (size_x + 9) // 4)
    in_chunks(begin, chunks, 4, material)
    load_z()
    in_chunks(0, some, 2, unpack((1, 2, 3)))

    def start(values, chosen):
        parts = z_parts(values)
        for at in chosen:
            modes = tile_modes(parts, at)
            for number, key in enumerate(KEYS):
                held[number, at * PAD : (at + 1) * PAD] = modes[key]

    start([field[comp + 1, begin + 2] for comp in range(3)], all_tiles)
    carry[...] = jnp.zeros_like(carry)

    def operate(chunk):
        parts = [z_parts([field[comp + 1, step + 3] for comp in range(3)]) for step in chunk]
        moved = [{} for _ in chunk]
        stays = [{} for _ in chunk]
        for at in all_tiles:
            spot = slice(at * PAD, (at + 1) * PAD)
            old = {key: held[number, spot] for number, key in enumerate(KEYS)}
            above = {key: carry[number, spot] for number, key in enumerate(KEYS)}
            for place, step in enumerate(chunk):
                new = tile_modes(parts[place], at)
                forces = modal_product(modal, element_modes(old, new))
                old = new
                stiff = moduli[step, spot]
                at_node = {}
                for key in KEYS:
                    even, odd = forces[key_row(0, key)], forces[key_row(1, key)]
                    odd = odd * stiff
                    if even is None:
                        at_node[key] = above[key] - odd
                        above[key] = odd
                    else:
                        even = even * stiff
                        at_node[key] = above[key] + (even - odd)
                        above[key] = even + odd
                for comp, mode_z in itertools.product(range(3), range(2)):
                    even, odd = at_node[(comp, 0, mode_z)], at_node[(comp, 1, mode_z)]
                    moved[place].setdefault((comp, mode_z), []).append(even + odd)
                    stays[place].setdefault((comp, mode_z), []).append(even - odd)
            for number, key in enumerate(KEYS):
                held[number, spot] = old[key]
                carry[number, spot] = above[key]
        for place, step in enumerate(chunk):
            known = inside_x(step - 3)
            for comp in range(3):
                totals = []
                for at in all_tiles:
                    spot = slice(at * PAD, (at + 1) * PAD)
                    along = [
                        stays[place][(comp, mode_z)][at]
                        + shift_tile(moved[place][(comp, mode_z)], at, 1)
                        for mode_z in range(2)
                    ]
                    total = (along[0] - along[1]) + roll(along[0] + along[1], 1)
                    total = total + spring_rate * field[comp + 1, step + 2, spot]
                    totals.append(total * (masks[0, spot] * known))
                total = jnp.concatenate(totals, 0)
                applied[comp, step, :rows] = patched(total, count_t)
                applied[comp, step, rows:] = totals[-1]

    in_chunks(begin, chunks, 4, operate)

    start([applied[comp, 3] for comp in range(3)], own_tiles)

    def products(number, sums):
        rr, rs, ss, es = sums
        chunk = [number * 4 + at for at in range(4)]
        parts = [z_parts([applied[comp, step + 4] for comp in range(3)]) for step in chunk]
        for step, comp in itertools.product(chunk, range(3)):
            res = field[comp + 1, step + HALO, :size_y]
            app = applied[comp, step + 3, :size_y]
            rr, rs, ss = rr + res * res, rs + res * app, ss + app * app
        strain = tiles_of(es)
        for number, at in enumerate(own_tiles):
            spot = slice(at * PAD, (at + 1) * PAD)
            old = {key: held[number, spot] for number, key in enumerate(KEYS)}
            for place, step in enumerate(chunk):
                new = tile_modes(parts[place], at)
                energy = modal_energy(modal, element_modes(old, new))
                old = new
                strain[number] = strain[number] + energy * moduli[step + 3, spot]
            for key_number, key in enumerate(KEYS):
                held[key_number, spot] = old[key]
        return rr, rs, ss, jnp.concatenate(strain, 0)

    nothing = jnp.zeros((size_y, size_z), f32)
    most = jnp.zeros((size_y + PAD, size_z), f32)
    sums = list(lax.fori_loop(0, size_x // 4, products, (nothing, nothing, nothing, most)))
    lane_main = lax.broadcasted_iota(jnp.int32, (size_y, lanes), 1)
    strain = jnp.where(lane_main < size_z - 1, sums[3][:size_y], 0.0)
    ends = (in_group == 3 * PAD - 1) & (lane_of < size_y // PAD * group)
    sums[3] = jnp.concatenate([strain, jnp.where(ends, sums[3][size_y:], 0.0)], 0)
    row8 = lax.broadcasted_iota(jnp.int32, (8, LANES), 0)
    tile = jnp.zeros((8, LANES), f32)
    for number, value in enumerate(sums):
        line = jnp.sum(value, axis=0, keepdims=True)
        tile = jnp.where(row8 == number, line, tile)

    def all_sum(slots, partner, count, send, recv):
        copies = [
            pltpu.make_async_remote_copy(
                src_ref=slots.at[0], dst_ref=slots.at[step], send_sem=send.at[step],
                recv_sem=recv.at[step], device_id=partner(step), device_id_type=MESH,
            )
            for step in range(1, count)
        ]
        for copy in copies:
            copy.start()
        total = slots[0]
        for step, copy in enumerate(copies):
            copy.wait_recv()
            total = total + slots[step + 1]
        for copy in copies:
            copy.wait_send()
        return total

    part_z[0] = tile
    part_xy[0] = all_sum(part_z, z_partner, count_z, z_send, z_recv)
    total = all_sum(part_xy, xy_partner, count_x * count_y, xy_send, xy_recv)
    total = jnp.sum(total, axis=1, keepdims=True)
    rr, rs, ss, es = (total[number : number + 1] for number in range(4))
    st = es + spring_rate * ss
    step_first = rr / rs
    rr_next = step_first * step_first * ss - rr
    product = rs - 2.0 * step_first * ss + step_first * step_first * st
    ratio = rr_next / rr
    step_second = rr_next / (product - ratio * rr_next / step_first)
    by_load = step_first + step_second * (1.0 + ratio)
    by_applied = -step_first * step_second

    def displaced(comp, plane):
        return by_load * field[comp + 1, plane + 2] + by_applied * applied[comp, plane]

    for far_x in range(3):
        for side, spot in ((first, 0), (last, size_x + 2)):

            @pl.when(side)
            def _():
                pushed[far_x, spot : spot + 2] = jnp.zeros((2, size_y + PAD, size_z), f32)

    start([displaced(comp, begin + 1) for comp in range(3)], all_tiles)

    def energies(chunk):
        parts = [z_parts([displaced(comp, step + 2) for comp in range(3)]) for step in chunk]
        pushes = [[] for _ in chunk]
        for at in all_tiles:
            spot = slice(at * PAD, (at + 1) * PAD)
            old = {key: held[number, spot] for number, key in enumerate(KEYS)}
            for place, step in enumerate(chunk):
                new = tile_modes(parts[place], at)
                energy = modal_energy(modal, element_modes(old, new))
                old = new
                pushes[place].append(energy * factor[step + 1, spot])
            for number, key in enumerate(KEYS):
                held[number, spot] = old[key]
        for place, step in enumerate(chunk):
            for number, sums in enumerate(cone_tiles(table, pushes[place], own_tiles)):
                for far_x in range(3):
                    pushed[far_x, step, number * PAD : (number + 1) * PAD] = sums[far_x]

    in_chunks(begin, jnp.where(at_side, (size_x + 7) // 6, (size_x + 9) // 6), 6, energies)

    def finish(chunk):
        for plane in chunk:
            sens_out[plane] = patched(gathered(pushed, plane + 2), count_t)
            for comp in range(3):
                disp_out[comp, plane] = displaced(comp, plane + 3)[:size_y]

    in_chunks(0, size_x // 4, 4, finish)


def solution(mesh):
    counts = tuple(mesh.shape[name] for name in ("gx", "gy", "gz"))
    placed = (P(None, "gx", "gy", "gz"), P("gx", "gy", "gz"), P())

    def body(load_field, design, solid_map):
        size_x, size_y, size_z = design.shape
        rows = size_y + 2 * PAD
        full, lanes = rows + PAD, size_z
        planes = size_x + 2 * HALO
        f32 = jnp.float32
        vmem = pl.BlockSpec(memory_space=pltpu.VMEM)
        anywhere = pl.BlockSpec(memory_space=pltpu.HBM)
        pairs = counts[0] * counts[1]
        dma = pltpu.SemaphoreType.DMA

        def run(*refs):
            kernel(counts, *refs)

        return pl.pallas_call(
            run,
            out_shape=(
                jax.ShapeDtypeStruct(load_field.shape, f32),
                jax.ShapeDtypeStruct(design.shape, f32),
                jax.ShapeDtypeStruct(design.shape, f32),
            ),
            in_specs=[anywhere, anywhere, pl.BlockSpec(memory_space=pltpu.SMEM)],
            out_specs=(vmem, vmem, vmem),
            scratch_shapes=[
                pltpu.VMEM((4, planes + 2, full, lanes), f32),
                pltpu.VMEM((3, size_x + 10, full, lanes), f32),
                pltpu.VMEM((size_x + 10, full, lanes), f32),
                pltpu.VMEM((size_x + 10, full, lanes), f32),
                pltpu.VMEM((size_x // BRICK + 2, full, lanes), f32),
                pltpu.VMEM((3, planes + 6, full, lanes), f32),
                pltpu.VMEM((3, size_x + 8, size_y + PAD, size_z), f32),
                pltpu.VMEM((12, full, lanes), f32),
                pltpu.VMEM((12, full, lanes), f32),
                pltpu.VMEM((4, planes, PAD, LANES), f32),
                pltpu.VMEM((2, 4, planes, PAD, LANES), f32),
                pltpu.VMEM((4, full, lanes), f32),
                pltpu.VMEM((counts[2], 8, LANES), f32),
                pltpu.VMEM((pairs, 8, LANES), f32),
                dma((12,)),
                dma((12,)),
                dma((counts[2],)),
                dma((counts[2],)),
                dma((pairs,)),
                dma((pairs,)),
                dma((4,)),
            ],
            compiler_params=pltpu.CompilerParams(
                collective_id=0, has_side_effects=True, vmem_limit_bytes=40 * 2**20
            ),
        )(load_field, design, solid_map)

    return jax.shard_map(
        body,
        mesh=mesh,
        in_specs=placed,
        out_specs=(P(None, "gx", "gy", "gz"), P("gx", "gy", "gz"), P("gx", "gy", "gz")),
        check_vma=False,
    )
```
